256 devices in a mesh: ctx: 32 (over z_hi, y, core), ch: 8 (over x, z_lo).
Axes of the slice: x: 4, y: 4, z: 8 (z_hi: 4, z_lo: 2; z = z_hi * 2 + z_lo), core: 2. Of those that a mesh axis runs over, the one named last changes fastest.
Arguments:
- inputs: float32 [24576, 2048], P('ctx', 'ch'), may hold values from -6 to 6
- cotangent: float32 [24576, 2048], P('ctx', 'ch'), may hold values from -6 to 6
- filter_rows: float32 [1536, 2048], P('ctx', 'ch'), may hold values from -0.15625 to 0.15625
- skip_gain: float32 [2048], P('ch'), may hold values from -1 to 1
- band_blocks: int32 [2048], P('ch'), may hold values from 1 to 2
Outputs:
- outputs: float32 [24576, 2048], P('ctx', 'ch')
- input_grad: float32 [2048, 24576], P(('ch', 'ctx'))
The draws below stay inside these ranges and needn't reach their ends.
All inputs are finite; a program needn't handle non-finite values.
Results may differ from the reference program's by a relative error of at most 0.00007.
Values sent between devices are 32-bit elements; how exact they have to be, the bound alone decides.
No kernel may reach another device: no remote copies, remote signals or barrier semaphores. Data moves between devices by JAX's collectives and lax.ppermute only.
A program may use at most 128 MiB of HBM per device.

```python
import jax
import jax.numpy as jnp
from jax import lax

CH = 2048
BLK = 768
MAXB = 2
TOKENS = 24576
CH_DEV = 256


def draw_band_blocks(key, part):
    groups = CH // CH_DEV
    key_cap, key_pick, key_each, key_slot = jax.random.split(key, 4)
    group_cap = jax.random.randint(key_cap, (groups,), 1, MAXB + 1)
    chosen = jax.random.randint(key_pick, (), 0, groups)
    group_ids = jnp.arange(groups, dtype=jnp.int32)
    group_cap = jnp.where(group_ids == chosen, MAXB, group_cap)
    raw_draw = jax.random.randint(key_each, (groups, CH_DEV), 0, MAXB * 8)
    band_vals = 1 + raw_draw % group_cap[:, None]
    slot_pos = jax.random.randint(key_slot, (), 0, CH_DEV)
    slot_ids = jnp.arange(CH_DEV, dtype=jnp.int32)
    in_chosen = group_ids[:, None] == chosen
    high_mask = in_chosen & (slot_ids[None, :] == slot_pos)
    low_mask = in_chosen & (slot_ids[None, :] == (slot_pos + 1) % CH_DEV)
    band_vals = jnp.where(high_mask, MAXB, jnp.where(low_mask, 1, band_vals))
    return band_vals.reshape(CH).astype(jnp.int32)


def block_levels(own_key, dims, pieces, low, high):
    def one(axis_at, parts):
        heights = jax.random.uniform(jax.random.fold_in(jax.random.fold_in(own_key, 6), axis_at), (parts,), jnp.float32, low / len(pieces), high / len(pieces))
        return jnp.repeat(jnp.exp(heights), dims[axis_at] // parts).reshape((-1,) + (1,) * (len(dims) - axis_at - 1))

    gain = one(*pieces[0])
    for cut in pieces[1:]:
        gain = gain * one(*cut)
    return gain


def noise(stream_key, extent, spread, limit, cuts=(), held_as=jnp.bfloat16):
    factor_of = block_levels(stream_key, extent, cuts, -0.22, 0.18) if cuts else 1.0
    result = jax.random.normal(stream_key, extent, jnp.float32) * spread * factor_of
    return jnp.minimum(jnp.maximum(result, -limit), limit).astype(held_as)


def setup_inputs(seed: int = 0) -> dict:
    arg_keys = jax.random.split(jax.random.key(seed), 6)
    return {
        "inputs": noise(arg_keys[0], (TOKENS, CH), 1.0, 6.0, ((0, 32), (1, 8)), jnp.float32),
        "cotangent": noise(arg_keys[1], (TOKENS, CH), 1.0, 6.0, ((0, 32), (1, 8)), jnp.float32),
        "filter_rows": noise(arg_keys[2], (MAXB * BLK, CH), (MAXB * BLK) ** -0.5, 0.15625, ((0, 32), (1, 8)), jnp.float32),
        "skip_gain": jnp.clip(jax.random.uniform(arg_keys[3], (CH,), jnp.float32, -1.0, 1.0) * block_levels(arg_keys[3], (CH,), ((0, 8),), -0.4, 0.0), -1.0, 1.0),
        "band_blocks": draw_band_blocks(jax.random.fold_in(arg_keys[5], 71), 0),
    }


def reference(inputs, cotangent, filter_rows, skip_gain, band_blocks):
    lag_index = jnp.arange(MAXB * BLK, dtype=jnp.int32)
    keep_mask = lag_index[:, None] < band_blocks[None, :] * BLK
    filter_full = jnp.where(keep_mask, filter_rows, jnp.zeros_like(filter_rows))
    length = 2 * TOKENS
    groups = CH // CH_DEV

    def per_group(packed):
        signal, grad_in, tap_rows, gain_row = packed
        spec_taps = jnp.fft.rfft(tap_rows, n=length, axis=0)
        spec_signal = jnp.fft.rfft(signal, n=length, axis=0)
        spec_grad = jnp.fft.rfft(grad_in, n=length, axis=0)
        forward_part = jnp.fft.irfft(spec_taps * spec_signal, n=length, axis=0)[:TOKENS]
        backward_part = jnp.fft.irfft(jnp.conj(spec_taps) * spec_grad, n=length, axis=0)[:TOKENS]
        forward_part = forward_part + gain_row[None, :] * signal
        backward_part = backward_part + gain_row[None, :] * grad_in
        return forward_part, backward_part.T

    stacked = (
        inputs.reshape(TOKENS, groups, CH_DEV).transpose(1, 0, 2),
        cotangent.reshape(TOKENS, groups, CH_DEV).transpose(1, 0, 2),
        filter_full.reshape(MAXB * BLK, groups, CH_DEV).transpose(1, 0, 2),
        skip_gain.reshape(groups, CH_DEV),
    )
    forward_all, backward_all = lax.map(per_group, stacked)
    outputs = forward_all.transpose(1, 0, 2).reshape(TOKENS, CH)
    input_grad = backward_all.reshape(CH, TOKENS)
    return outputs, input_grad
```

```python
import jax
import jax.numpy as jnp
from jax import lax
from jax.experimental import pallas as pl
from jax.experimental.pallas import tpu as pltpu
from jax.sharding import PartitionSpec as P

LANES = 128
SUBS = 8


def tap_tile(taps_ref, gain_ref, band_ref, block_len):
    rows, chans = taps_ref.shape
    lag = lax.axis_index("ctx") * rows + lax.broadcasted_iota(jnp.int32, (rows, chans), 0)
    kept = jnp.where(lag < band_ref[...] * block_len, taps_ref[...], 0.0)
    kept = kept + jnp.where(lag == 0, gain_ref[...], 0.0)
    return jnp.concatenate([kept, jnp.zeros((LANES - rows, chans), jnp.float32)], axis=0).T


def pack_with_taps(x_ref, taps_ref, gain_ref, band_ref, out_ref):
    tiles = x_ref.shape[0] // LANES
    for k in range(tiles):
        part = x_ref[k * LANES:(k + 1) * LANES, :].T
        out_ref[:, k, :, :] = part.reshape(-1, SUBS, LANES)
    part = tap_tile(taps_ref, gain_ref, band_ref, x_ref.shape[0])
    out_ref[:, tiles, :, :] = part.reshape(-1, SUBS, LANES)


def pack_plain(x_ref, out_ref):
    for k in range(x_ref.shape[0] // LANES):
        part = x_ref[k * LANES:(k + 1) * LANES, :].T
        out_ref[:, k, :, :] = part.reshape(-1, SUBS, LANES)


def unpack(y_ref, out_ref):
    for k in range(out_ref.shape[0] // LANES):
        part = y_ref[:, k, :, :].reshape(-1, LANES)
        out_ref[k * LANES:(k + 1) * LANES, :] = part.T


def split(value):
    high = value.astype(jnp.bfloat16)
    return high, (value - high.astype(jnp.float32)).astype(jnp.bfloat16)


def lay_taps(read_piece, pieces, rows, lag_tiles, row_ref):
    lane = lax.broadcasted_iota(jnp.int32, (SUBS, LANES), 1)
    held = [jnp.zeros((SUBS, LANES), jnp.float32) for _ in range(lag_tiles + 2)]
    for piece in range(pieces):
        tile, offset = divmod(LANES + rows * piece, LANES)
        value = read_piece(piece)
        turned = pltpu.roll(value, offset, axis=1) if offset else value
        if offset + rows <= LANES:
            held[tile] = held[tile] + turned
        else:
            held[tile] = held[tile] + jnp.where(lane >= offset, turned, 0.0)
            held[tile + 1] = held[tile + 1] + jnp.where(lane < offset, turned, 0.0)
    for tile in range(lag_tiles + 2):
        row_ref[:, tile * LANES:(tile + 1) * LANES] = held[tile]


def toeplitz(row_ref, chan):
    row = row_ref[pl.ds(chan, 1), :]
    wide = jnp.broadcast_to(row, (LANES, row.shape[1]))
    return pltpu.roll(wide, 0, axis=1, stride=1, stride_axis=0)[:, LANES:]


def shifted(value, steps):
    if steps == 0:
        return value
    blank = jnp.zeros((abs(steps), value.shape[1]), value.dtype)
    if steps > 0:
        return jnp.concatenate([blank, value[:-steps]], axis=0)
    return jnp.concatenate([value[-steps:], blank], axis=0)


def convolve(signal_ref, signal_tiles, taps_ref, taps_tiles, put, row_ref, blocks, tiles, rows, lag_tiles, backward):
    chunk = signal_tiles * SUBS
    tap_chunk = taps_tiles * SUBS

    def read_piece(piece):
        base = piece * tap_chunk + (taps_tiles - 1) * SUBS
        return taps_ref[base:base + SUBS, :]

    lay_taps(read_piece, blocks, rows, lag_tiles, row_ref)
    depth = lag_tiles + 1
    sign = -1 if backward else 1

    def one(chan, carry):
        high_t, low_t = split(toeplitz(row_ref, chan))
        moved = {}
        for k in range(tiles):
            value = signal_ref[pl.ds(k * SUBS + chan, blocks, stride=chunk), :]
            for steps in range(3):
                high, low = split(shifted(value, sign * steps))
                moved[k, steps] = jnp.concatenate([high, low], axis=0)
        columns = []
        for d in range(depth):
            parts = []
            for k in range(tiles):
                turns, at = divmod(k - sign * d, tiles)
                parts.append(moved[at, abs(turns)])
            columns.append(jnp.concatenate(parts, axis=0))
        left = jnp.concatenate(columns, axis=1)
        if backward:
            right = jnp.concatenate([high_t, low_t], axis=0)
            total = lax.dot_general(left, right, (((1,), (1,)), ((), ())), preferred_element_type=jnp.float32)
        else:
            right = jnp.concatenate(
                [jnp.concatenate([t[:, d * LANES:(d + 1) * LANES] for t in (high_t, low_t)], axis=1) for d in range(depth)],
                axis=0,
            )
            total = jnp.dot(left, right, preferred_element_type=jnp.float32)
        total = total[:, :LANES] + total[:, LANES:]
        for k in range(tiles):
            base = 2 * blocks * k
            put(k, chan, total[base:base + blocks] + total[base + blocks:base + 2 * blocks])
        return carry

    lax.fori_loop(0, SUBS, one, 0)


def forward(blocks, tiles, rows, lag_tiles, x_ref, y_ref, row_ref):
    def put(k, chan, value):
        y_ref[pl.ds(k * SUBS + chan, blocks, stride=tiles * SUBS), :] = value

    convolve(x_ref, tiles + 1, x_ref, tiles + 1, put, row_ref, blocks, tiles, rows, lag_tiles, False)


def gradient(blocks, tiles, rows, lag_tiles, g_ref, x_ref, out_ref, row_ref, held_ref):
    def put(k, chan, value):
        held_ref[pl.ds(k * SUBS + chan, blocks, stride=tiles * SUBS), :] = value

    convolve(g_ref, tiles, x_ref, tiles + 1, put, row_ref, blocks, tiles, rows, lag_tiles, True)
    for tile in range(blocks * tiles):
        out_ref[:, tile * LANES:(tile + 1) * LANES] = held_ref[tile * SUBS:(tile + 1) * SUBS, :]


def call(body, shape, scratch=(), flops=0, moved=0):
    return pl.pallas_call(
        body,
        out_shape=jax.ShapeDtypeStruct(shape, jnp.float32),
        scratch_shapes=list(scratch),
        compiler_params=pltpu.CompilerParams(vmem_limit_bytes=40 * 1024 * 1024),
        cost_estimate=pl.CostEstimate(flops=flops, bytes_accessed=moved, transcendentals=0),
    )


def local(inputs, cotangent, filter_rows, skip_gain, band_blocks):
    count = lax.axis_size("ctx")
    block_len, chans = inputs.shape
    rows = filter_rows.shape[0]
    tiles = block_len // LANES
    lag_tiles = rows * count // LANES
    size = block_len * chans * 4

    def exchanged(value):
        return lax.all_to_all(value, "ctx", split_axis=0, concat_axis=0, tiled=True)

    sent_x = call(pack_with_taps, (count, tiles + 1, SUBS, LANES), moved=2 * size)(
        inputs, filter_rows, skip_gain[None, :], band_blocks[None, :])
    got_x = exchanged(sent_x).reshape(-1, LANES)
    sent_g = call(pack_plain, (count, tiles, SUBS, LANES), moved=2 * size)(cotangent)
    got_g = exchanged(sent_g).reshape(-1, LANES)
    row = pltpu.VMEM((SUBS, (lag_tiles + 2) * LANES), jnp.float32)
    flops = 2 * SUBS * 2 * count * tiles * (lag_tiles + 1) * LANES * 2 * LANES
    sizes = (count, tiles, rows, lag_tiles)
    sent_y = call(lambda *refs: forward(*sizes, *refs), (count * tiles * SUBS, LANES), [row], flops, 2 * size)(got_x)
    got_y = exchanged(sent_y.reshape(count, tiles, SUBS, LANES))
    held = pltpu.VMEM((count * tiles * SUBS, LANES), jnp.float32)
    input_grad = call(lambda *refs: gradient(*sizes, *refs), (SUBS, count * block_len), [row, held], flops, 3 * size)(
        got_g, got_x)
    outputs = call(unpack, (block_len, chans), moved=2 * size)(got_y)
    return outputs, input_grad


def solution(mesh):
    return jax.shard_map(
        local,
        mesh=mesh,
        in_specs=(P("ctx", "ch"), P("ctx", "ch"), P("ctx", "ch"), P("ch"), P("ch")),
        out_specs=(P("ctx", "ch"), P(("ch", "ctx"), None)),
        check_vma=False,
    )
```

```python
import jax
import jax.numpy as jnp
from jax import lax
from jax.experimental import pallas as pl
from jax.experimental.pallas import tpu as pltpu
from jax.sharding import Mesh, PartitionSpec as P

LANES = 128
SUBS = 8
NEAR = 8


def store_parts(out_ref, k, part):
    far = out_ref.shape[1]
    step = part.shape[0] // far
    for z in range(far):
        out_ref[:, z, k, :, :] = part[z * step:(z + 1) * step].reshape(-1, SUBS, LANES)


def pack_with_taps(x_ref, taps_ref, gain_ref, band_ref, out_ref):
    block_len = x_ref.shape[0]
    tiles = block_len // LANES
    for k in range(tiles):
        store_parts(out_ref, k, x_ref[k * LANES:(k + 1) * LANES, :].T)
    rows, chans = taps_ref.shape
    place = lax.axis_index("far") * NEAR + lax.axis_index("near")
    lag = place * rows + lax.broadcasted_iota(jnp.int32, (rows, chans), 0)
    kept = jnp.where(lag < band_ref[...] * block_len, taps_ref[...], 0.0)
    kept = kept + jnp.where(lag == 0, gain_ref[...], 0.0)
    kept = jnp.concatenate([kept, jnp.zeros((LANES - rows, chans), jnp.float32)], axis=0)
    store_parts(out_ref, tiles, kept.T)


def pack_plain(x_ref, out_ref):
    for k in range(x_ref.shape[0] // LANES):
        part = x_ref[k * LANES:(k + 1) * LANES, :].T
        out_ref[:, k, :, :] = part.reshape(-1, SUBS, LANES)


def unpack(y_ref, out_ref):
    for k in range(out_ref.shape[0] // LANES):
        part = jnp.concatenate([y_ref[:, z, k, :, :].reshape(-1, LANES) for z in range(y_ref.shape[1])], axis=0)
        out_ref[k * LANES:(k + 1) * LANES, :] = part.T


def split(value):
    high = value.astype(jnp.bfloat16)
    return high, (value - high.astype(jnp.float32)).astype(jnp.bfloat16)


def collect(rows, halo_blocks, x_ref, halo_ref, taps_ref):
    near, far, tiles = x_ref.shape[:3]
    tiles = tiles - 1
    lane = lax.broadcasted_iota(jnp.int32, (far * SUBS, LANES), 1)
    own_tiles = rows * near // LANES
    held = [jnp.zeros((far * SUBS, LANES), jnp.float32) for _ in range(own_tiles)]
    for piece in range(near):
        tile, offset = divmod(rows * piece, LANES)
        value = x_ref[piece, :, tiles, :, :].reshape(far * SUBS, LANES)
        turned = pltpu.roll(value, offset, axis=1) if offset else value
        if offset + rows <= LANES:
            held[tile] = held[tile] + turned
        else:
            held[tile] = held[tile] + jnp.where(lane >= offset, turned, 0.0)
            held[tile + 1] = held[tile + 1] + jnp.where(lane < offset, turned, 0.0)
    height = far * SUBS
    halo_rows = halo_blocks * far * tiles * SUBS
    for tile in range(own_tiles):
        taps_ref[tile * height:(tile + 1) * height, :] = held[tile]
        halo_ref[halo_rows + tile * height:halo_rows + (tile + 1) * height, :] = held[tile]
    for block in range(halo_blocks):
        for z in range(far):
            base = (block * far + z) * tiles * SUBS
            halo_ref[base:base + tiles * SUBS, :] = x_ref[near - halo_blocks + block, z, :tiles, :, :].reshape(-1, LANES)


def toeplitz(row):
    wide = jnp.broadcast_to(row, (LANES, row.shape[1]))
    return pltpu.roll(wide, 0, axis=1, stride=1, stride_axis=0)[:, LANES:]


def shifted(value, steps):
    if steps == 0:
        return value
    blank = jnp.zeros((steps, value.shape[1]), value.dtype)
    return jnp.concatenate([value[steps:], blank], axis=0)


def lay_rows(row_ref, pieces, count, height, rows_of):
    per = (row_ref.shape[0] - 2) // count
    row_ref[0] = jnp.zeros(row_ref.shape[1:], jnp.float32)
    row_ref[row_ref.shape[0] - 1] = jnp.zeros(row_ref.shape[1:], jnp.float32)
    me = lax.axis_index("far")
    for back, (ref, base) in enumerate(pieces):
        source = lax.rem(me + count - back, count)
        for tile in range(per):
            row_ref[1 + source * per + tile] = rows_of(ref, base + tile * height)


def row_of(row_ref, chan):
    return jnp.concatenate([row_ref[t, pl.ds(chan, 1), :] for t in range(row_ref.shape[0])], axis=1)


def forward(halo_blocks, tiles, x_ref, halo_ref, *refs):
    others, (y_ref, row_ref, held_ref) = refs[:-3], refs[-3:]
    far = len(others) + 1
    chans = far * SUBS
    near = y_ref.shape[0] // (far * tiles * SUBS)
    chunk = far * (tiles + 1) * SUBS
    halo_rows = halo_blocks * far * tiles * SUBS
    pieces = [(others[0], 0), (halo_ref, halo_rows)] + [(ref, 0) for ref in others[1:]]
    lay_rows(row_ref, pieces, far, chans, lambda ref, base: ref[base:base + chans, :])
    first = lax.axis_index("far") == 0
    for block in range(halo_blocks):
        for z in range(far):
            source = (block * far + z) * tiles * SUBS
            target = block * chunk + z * (tiles + 1) * SUBS
            value = halo_ref[source:source + tiles * SUBS, :]
            held_ref[target:target + tiles * SUBS, :] = jnp.where(first, 0.0, value)
    held_ref[halo_blocks * chunk:, :] = x_ref[...]
    depth = row_ref.shape[0] - 1

    def one(chan, carry):
        z, i = lax.div(chan, SUBS), lax.rem(chan, SUBS)
        high_t, low_t = split(toeplitz(row_of(row_ref, chan)))
        moved = {}
        for k in range(tiles):
            for steps in range(halo_blocks + 1):
                start = (halo_blocks - steps) * chunk + z * (tiles + 1) * SUBS + k * SUBS + i
                moved[k, steps] = jnp.concatenate(split(held_ref[pl.ds(start, near, stride=chunk), :]), axis=0)
        columns = []
        for d in range(depth):
            parts = []
            for k in range(tiles):
                turns, at = divmod(k - d, tiles)
                parts.append(moved[at, -turns])
            columns.append(jnp.concatenate(parts, axis=0))
        left = jnp.concatenate(columns, axis=1)
        right = jnp.concatenate(
            [jnp.concatenate([t[:, d * LANES:(d + 1) * LANES] for t in (high_t, low_t)], axis=1) for d in range(depth)],
            axis=0,
        )
        total = jnp.dot(left, right, preferred_element_type=jnp.float32)
        total = total[:, :LANES] + total[:, LANES:]
        for k in range(tiles):
            base = 2 * near * k
            value = total[base:base + near] + total[base + near:base + 2 * near]
            y_ref[pl.ds((z * tiles + k) * SUBS + i, near, stride=far * tiles * SUBS), :] = value
        return carry

    lax.fori_loop(0, chans, one, 0)


def gradient(blocks, tiles, halo_rows, g_ref, halo_ref, *refs):
    others, (out_ref, row_ref, held_ref) = refs[:-3], refs[-3:]
    far = len(others) + 1
    me = lax.axis_index("far")
    pieces = [(others[0], 0), (halo_ref, halo_rows)] + [(ref, 0) for ref in others[1:]]
    lay_rows(row_ref, pieces, far, far * SUBS,
             lambda ref, base: ref[pl.ds(pl.multiple_of(base + me * SUBS, SUBS), SUBS), :])
    depth = row_ref.shape[0] - 1
    chunk = tiles * SUBS

    def one(chan, carry):
        high_t, low_t = split(toeplitz(row_of(row_ref, chan)))
        moved = {}
        for k in range(tiles):
            value = g_ref[pl.ds(k * SUBS + chan, blocks, stride=chunk), :]
            for steps in range((depth + tiles - 2) // tiles + 1):
                moved[k, steps] = jnp.concatenate(split(shifted(value, steps)), axis=0)
        columns = []
        for d in range(depth):
            parts = []
            for k in range(tiles):
                turns, at = divmod(k + d, tiles)
                parts.append(moved[at, turns])
            columns.append(jnp.concatenate(parts, axis=0))
        left = jnp.concatenate(columns, axis=1)
        right = jnp.concatenate([high_t, low_t], axis=0)
        total = lax.dot_general(left, right, (((1,), (1,)), ((), ())), preferred_element_type=jnp.float32)
        total = total[:, :LANES] + total[:, LANES:]
        for k in range(tiles):
            base = 2 * blocks * k
            value = total[base:base + blocks] + total[base + blocks:base + 2 * blocks]
            held_ref[pl.ds(k * SUBS + chan, blocks, stride=chunk), :] = value
        return carry

    lax.fori_loop(0, SUBS, one, 0)
    for tile in range(blocks * tiles):
        out_ref[:, tile * LANES:(tile + 1) * LANES] = held_ref[tile * SUBS:(tile + 1) * SUBS, :]


def call(body, shapes, scratch=(), flops=0, moved=0):
    shapes = [jax.ShapeDtypeStruct(shape, jnp.float32) for shape in shapes]
    return pl.pallas_call(
        body,
        out_shape=shapes if len(shapes) > 1 else shapes[0],
        scratch_shapes=list(scratch),
        compiler_params=pltpu.CompilerParams(vmem_limit_bytes=40 * 1024 * 1024),
        cost_estimate=pl.CostEstimate(flops=flops, bytes_accessed=moved, transcendentals=0),
    )


def local(inputs, cotangent, filter_rows, skip_gain, band_blocks):
    far = lax.axis_size("far")
    near = lax.axis_size("near")
    count = far * near
    block_len, chans = inputs.shape
    rows = filter_rows.shape[0]
    tiles = block_len // LANES
    lag_tiles = rows * count // LANES
    halo_blocks = rows * count // block_len
    size = block_len * chans * 4

    def exchanged(value, axes):
        return lax.all_to_all(value, axes, split_axis=0, concat_axis=0, tiled=True)

    def ahead(value, steps):
        return lax.ppermute(value, "far", [(z, (z + steps) % far) for z in range(far)])

    sent_x = call(pack_with_taps, [(near, far, tiles + 1, SUBS, LANES)], moved=2 * size)(
        inputs, filter_rows, skip_gain[None, :], band_blocks[None, :])
    got_x = exchanged(sent_x, "near")
    halo_rows = halo_blocks * far * tiles * SUBS
    own_taps = lag_tiles // far * far * SUBS
    halo, taps = call(lambda *refs: collect(rows, halo_blocks, *refs),
                      [(halo_rows + own_taps, LANES), (own_taps, LANES)], moved=size)(got_x)
    got_halo = ahead(halo, 1)
    pieces = [taps] + [ahead(taps, steps) for steps in range(2, far)]
    sent_g = call(pack_plain, [(count, tiles, SUBS, LANES)], moved=2 * size)(cotangent)
    got_g = exchanged(sent_g, ("far", "near")).reshape(-1, LANES)

    def row(height):
        return pltpu.VMEM((lag_tiles + 2, height, LANES), jnp.float32)

    got_x = got_x.reshape(-1, LANES)
    held_rows = (near + halo_blocks) * far * (tiles + 1) * SUBS
    flops = 2 * far * SUBS * 2 * near * tiles * (lag_tiles + 1) * LANES * 2 * LANES
    sent_y = call(lambda *refs: forward(halo_blocks, tiles, *refs), [(count * tiles * SUBS, LANES)],
                  [row(far * SUBS), pltpu.VMEM((held_rows, LANES), jnp.float32)], 4 * flops, 2 * size)(
        got_x, got_halo, *pieces)
    got_y = exchanged(sent_y.reshape(near, far, tiles, SUBS, LANES), "near")
    input_grad = call(lambda *refs: gradient(count, tiles, halo_rows, *refs), [(SUBS, count * block_len)],
                      [row(SUBS), pltpu.VMEM((count * tiles * SUBS, LANES), jnp.float32)], flops, 3 * size)(
        got_g, got_halo, *pieces)
    outputs = call(unpack, [(block_len, chans)], moved=2 * size)(got_y)
    return outputs, input_grad


def solution(mesh):
    count, width = mesh.devices.shape
    fine = Mesh(mesh.devices.reshape(count // NEAR, NEAR, width), ("far", "near", "ch"))
    tokens = ("far", "near")
    return jax.shard_map(
        local,
        mesh=fine,
        in_specs=(P(tokens, "ch"), P(tokens, "ch"), P(tokens, "ch"), P("ch"), P("ch")),
        out_specs=(P(tokens, "ch"), P(("ch", "far", "near"), None)),
        check_vma=False,
    )
```

```python
import jax
import jax.numpy as jnp
from jax import lax
from jax.experimental import pallas as pl
from jax.experimental.pallas import tpu as pltpu
from jax.sharding import Mesh, PartitionSpec as P

LANES = 128
SUBS = 8
NEAR = 8


def store_parts(out_ref, k, part):
    far = out_ref.shape[1]
    step = part.shape[0] // far
    for z in range(far):
        out_ref[:, z, k, :, :] = part[z * step:(z + 1) * step].reshape(-1, SUBS, LANES)


def pack_with_taps(x_ref, gain_ref, band_ref, *refs):
    taps_refs, out_ref = refs[:-1], refs[-1]
    block_len = x_ref.shape[0]
    tiles = block_len // LANES
    for k in range(tiles):
        store_parts(out_ref, k, x_ref[k * LANES:(k + 1) * LANES, :].T)
    rows, chans = taps_refs[0].shape
    far = len(taps_refs)
    room = LANES // 2
    blank = jnp.zeros((room - rows, chans), jnp.float32)
    columns = []
    for back, taps_ref in enumerate(taps_refs):
        place = lax.rem(lax.axis_index("far") + far - back, far) * NEAR + lax.axis_index("near")
        lag = place * rows + lax.broadcasted_iota(jnp.int32, (rows, chans), 0)
        kept = jnp.where(lag < band_ref[...] * block_len, taps_ref[...], 0.0)
        columns += [kept + jnp.where(lag == 0, gain_ref[...], 0.0), blank]
    for tile in range(far // 2):
        store_parts(out_ref, tiles + tile, jnp.concatenate(columns[4 * tile:4 * tile + 4], axis=0).T)


def pack_plain(x_ref, after_ref, out_ref):
    for k in range(x_ref.shape[0] // LANES):
        part = x_ref[k * LANES:(k + 1) * LANES, :].T
        out_ref[:, k, :, :] = part.reshape(-1, SUBS, LANES)


def unpack(y_ref, after_ref, out_ref):
    for k in range(out_ref.shape[0] // LANES):
        part = jnp.concatenate([y_ref[:, z, k, :, :].reshape(-1, LANES) for z in range(y_ref.shape[1])], axis=0)
        out_ref[k * LANES:(k + 1) * LANES, :] = part.T


def split(value):
    high = value.astype(jnp.bfloat16)
    return high, (value - high.astype(jnp.float32)).astype(jnp.bfloat16)


def toeplitz(row):
    wide = jnp.broadcast_to(row, (LANES, row.shape[1]))
    return pltpu.roll(wide, 0, axis=1, stride=1, stride_axis=0)[:, LANES:]


def shifted(value, steps):
    if steps == 0:
        return value
    blank = jnp.zeros((steps, value.shape[1]), value.dtype)
    return jnp.concatenate([value[steps:], blank], axis=0)


def lay_rows(row_ref, taps_tiles, rows, near, far, piece_of):
    lane = lax.broadcasted_iota(jnp.int32, row_ref.shape[1:], 1)
    row_ref[...] = jnp.zeros(row_ref.shape, jnp.float32)
    room = LANES // 2
    per = rows * near // LANES
    for back in range(far):
        source = lax.rem(lax.axis_index("far") + far - back, far)
        for piece in range(near):
            tile, offset = divmod(rows * piece, LANES)
            value = piece_of(piece, back // 2)
            turn = (offset - room * (back % 2)) % LANES
            value = pltpu.roll(value, turn, axis=1) if turn else value
            at = 1 + source * per + tile
            row_ref[at] = row_ref[at] + jnp.where((lane >= offset) & (lane < offset + rows), value, 0.0)
            if offset + rows > LANES:
                row_ref[at + 1] = row_ref[at + 1] + jnp.where(lane < offset + rows - LANES, value, 0.0)


def row_of(row_ref, chan):
    return jnp.concatenate([row_ref[t, pl.ds(chan, 1), :] for t in range(row_ref.shape[0])], axis=1)


def forward(halo_blocks, tiles, rows, x_ref, halo_ref, y_ref, row_ref, held_ref):
    near, far, depth = x_ref.shape[:3]
    taps_tiles = depth - tiles
    chans = far * SUBS
    chunk = far * depth * SUBS
    lay_rows(row_ref, taps_tiles, rows, near, far,
             lambda piece, tile: x_ref[piece, :, tiles + tile, :, :].reshape(chans, LANES))
    first = lax.axis_index("far") == 0
    for block in range(halo_blocks):
        for z in range(far):
            at = block * chunk + z * depth * SUBS
            held_ref[at:at + tiles * SUBS, :] = jnp.where(first, 0.0, halo_ref[block, z].reshape(-1, LANES))
    held_ref[halo_blocks * chunk:, :] = x_ref[...].reshape(-1, LANES)
    each = depth * SUBS
    depth = row_ref.shape[0] - 1

    def one(chan, carry):
        z, i = lax.div(chan, SUBS), lax.rem(chan, SUBS)
        high_t, low_t = split(toeplitz(row_of(row_ref, chan)))
        moved = {}
        for k in range(tiles):
            for steps in range(halo_blocks + 1):
                start = (halo_blocks - steps) * chunk + z * each + k * SUBS + i
                moved[k, steps] = jnp.concatenate(split(held_ref[pl.ds(start, near, stride=chunk), :]), axis=0)
        columns = []
        for d in range(depth):
            parts = []
            for k in range(tiles):
                turns, at = divmod(k - d, tiles)
                parts.append(moved[at, -turns])
            columns.append(jnp.concatenate(parts, axis=0))
        left = jnp.concatenate(columns, axis=1)
        right = jnp.concatenate(
            [jnp.concatenate([t[:, d * LANES:(d + 1) * LANES] for t in (high_t, low_t)], axis=1) for d in range(depth)],
            axis=0,
        )
        total = jnp.dot(left, right, preferred_element_type=jnp.float32)
        total = total[:, :LANES] + total[:, LANES:]
        for k in range(tiles):
            base = 2 * near * k
            value = total[base:base + near] + total[base + near:base + 2 * near]
            y_ref[pl.ds((z * tiles + k) * SUBS + i, near, stride=far * tiles * SUBS), :] = value
        return carry

    lax.fori_loop(0, chans, one, 0)


def gradient(blocks, tiles, rows, g_ref, x_ref, out_ref, token_ref, row_ref, held_ref):
    token_ref[...] = jnp.zeros(token_ref.shape, jnp.float32)
    near, far = x_ref.shape[:2]
    me = lax.axis_index("far")
    lay_rows(row_ref, x_ref.shape[2] - tiles, rows, near, far,
             lambda piece, tile: x_ref[piece, me, tiles + tile, :, :])
    depth = row_ref.shape[0] - 1
    chunk = tiles * SUBS

    def one(chan, carry):
        high_t, low_t = split(toeplitz(row_of(row_ref, chan)))
        moved = {}
        for k in range(tiles):
            value = g_ref[pl.ds(k * SUBS + chan, blocks, stride=chunk), :]
            for steps in range((depth + tiles - 2) // tiles + 1):
                moved[k, steps] = jnp.concatenate(split(shifted(value, steps)), axis=0)
        columns = []
        for d in range(depth):
            parts = []
            for k in range(tiles):
                turns, at = divmod(k + d, tiles)
                parts.append(moved[at, turns])
            columns.append(jnp.concatenate(parts, axis=0))
        left = jnp.concatenate(columns, axis=1)
        right = jnp.concatenate([high_t, low_t], axis=0)
        total = lax.dot_general(left, right, (((1,), (1,)), ((), ())), preferred_element_type=jnp.float32)
        total = total[:, :LANES] + total[:, LANES:]
        for k in range(tiles):
            base = 2 * blocks * k
            value = total[base:base + blocks] + total[base + blocks:base + 2 * blocks]
            held_ref[pl.ds(k * SUBS + chan, blocks, stride=chunk), :] = value
        return carry

    lax.fori_loop(0, SUBS, one, 0)
    for tile in range(blocks * tiles):
        out_ref[:, tile * LANES:(tile + 1) * LANES] = held_ref[tile * SUBS:(tile + 1) * SUBS, :]


def call(body, shapes, scratch=(), flops=0, moved=0, operands=0, after=0):
    specs = [pl.BlockSpec(memory_space=pltpu.VMEM)] * operands + [pl.BlockSpec(memory_space=pl.ANY)] * after
    shapes = [jax.ShapeDtypeStruct(shape, jnp.float32) for shape in shapes]
    return pl.pallas_call(
        body,
        out_shape=shapes if len(shapes) > 1 else shapes[0],
        **({"in_specs": specs} if specs else {}),
        scratch_shapes=list(scratch),
        compiler_params=pltpu.CompilerParams(vmem_limit_bytes=40 * 1024 * 1024),
        cost_estimate=pl.CostEstimate(flops=flops, bytes_accessed=moved, transcendentals=0),
    )


def local(inputs, cotangent, filter_rows, skip_gain, band_blocks):
    far = lax.axis_size("far")
    near = lax.axis_size("near")
    count = far * near
    block_len, chans = inputs.shape
    rows = filter_rows.shape[0]
    tiles = block_len // LANES
    lag_tiles = rows * count // LANES
    halo_blocks = rows * count // block_len
    size = block_len * chans * 4

    def exchanged(value, axes):
        return lax.all_to_all(value, axes, split_axis=0, concat_axis=0, tiled=True)

    def ahead(value, steps):
        return lax.ppermute(value, "far", [(z, (z + steps) % far) for z in range(far)])

    taps = [filter_rows] + [ahead(filter_rows, steps) for steps in range(1, far)]
    depth = tiles + far // 2
    sent_x = call(pack_with_taps, [(near, far, depth, SUBS, LANES)], moved=2 * size)(
        inputs, skip_gain[None, :], band_blocks[None, :], *taps)
    got_x = exchanged(sent_x, "near")
    halo = got_x[near - halo_blocks:, :, :tiles]
    got_halo = ahead(halo, 1)
    sent_g = call(pack_plain, [(count, tiles, SUBS, LANES)], moved=2 * size, operands=1, after=1)(cotangent, halo)
    got_g = exchanged(sent_g, ("far", "near")).reshape(-1, LANES)

    def row(height):
        return pltpu.VMEM((lag_tiles + 2, height, LANES), jnp.float32)

    held_rows = (near + halo_blocks) * far * depth * SUBS
    flops = 2 * far * SUBS * 2 * near * tiles * (lag_tiles + 1) * LANES * 2 * LANES
    sent_y = call(lambda *refs: forward(halo_blocks, tiles, rows, *refs), [(count * tiles * SUBS, LANES)],
                  [row(far * SUBS), pltpu.VMEM((held_rows, LANES), jnp.float32)], 40 * flops, 2 * size)(
        got_x, got_halo)
    got_y = exchanged(sent_y.reshape(near, far, tiles, SUBS, LANES), "near")
    input_grad, token = call(lambda *refs: gradient(count, tiles, rows, *refs), [(SUBS, count * block_len), (SUBS, LANES)],
                      [row(SUBS), pltpu.VMEM((count * tiles * SUBS, LANES), jnp.float32)], flops, 3 * size)(
        got_g, got_x)
    outputs = call(unpack, [(block_len, chans)], moved=2 * size, operands=1, after=1)(got_y, token)
    return outputs, input_grad


def solution(mesh):
    count, width = mesh.devices.shape
    fine = Mesh(mesh.devices.reshape(count // NEAR, NEAR, width), ("far", "near", "ch"))
    tokens = ("far", "near")
    return jax.shard_map(
        local,
        mesh=fine,
        in_specs=(P(tokens, "ch"), P(tokens, "ch"), P(tokens, "ch"), P("ch"), P("ch")),
        out_specs=(P(tokens, "ch"), P(("ch", "far", "near"), None)),
        check_vma=False,
    )
```

```python
import jax
import jax.numpy as jnp
from jax import lax
from jax.experimental import pallas as pl
from jax.experimental.pallas import tpu as pltpu
from jax.sharding import Mesh, PartitionSpec as P

LANES = 128
SUBS = 8
NEAR = 8


def store_parts(out_ref, k, part):
    far = out_ref.shape[1]
    step = part.shape[0] // far
    for z in range(far):
        out_ref[:, z, k, :, :] = part[z * step:(z + 1) * step].reshape(-1, SUBS, LANES)


def pack_with_taps(x_ref, taps_ref, gain_ref, band_ref, out_ref):
    block_len = x_ref.shape[0]
    tiles = block_len // LANES
    for k in range(tiles):
        store_parts(out_ref, k, x_ref[k * LANES:(k + 1) * LANES, :].T)
    rows, chans = taps_ref.shape
    place = lax.axis_index("far") * NEAR + lax.axis_index("near")
    lag = place * rows + lax.broadcasted_iota(jnp.int32, (rows, chans), 0)
    kept = jnp.where(lag < band_ref[...] * block_len, taps_ref[...], 0.0)
    kept = kept + jnp.where(lag == 0, gain_ref[...], 0.0)
    kept = jnp.concatenate([kept, jnp.zeros((LANES - rows, chans), jnp.float32)], axis=0)
    store_parts(out_ref, tiles, kept.T)


def pack_by_far(g_ref, *refs):
    outs, held_ref = refs[:-1], refs[-1]
    far = len(outs)
    for k in range(g_ref.shape[0] // LANES):
        part = g_ref[k * LANES:(k + 1) * LANES, :].T
        step = part.shape[0] // far
        for z in range(far):
            held_ref[z, :, k, :, :] = part[z * step:(z + 1) * step].reshape(-1, SUBS, LANES)
    for steps, out_ref in enumerate(outs):
        out_ref[...] = held_ref[lax.rem(lax.axis_index("far") + steps, far)]


def stack(*refs):
    parts, out_ref = refs[:-1], refs[-1]
    far = len(parts)
    for back, ref in enumerate(parts):
        out_ref[:, lax.rem(lax.axis_index("far") + far - back, far)] = ref[...]


def unpack(y_ref, after_ref, out_ref):
    for k in range(out_ref.shape[0] // LANES):
        part = jnp.concatenate([y_ref[:, z, k, :, :].reshape(-1, LANES) for z in range(y_ref.shape[1])], axis=0)
        out_ref[k * LANES:(k + 1) * LANES, :] = part.T


def split(value):
    high = value.astype(jnp.bfloat16)
    return high, (value - high.astype(jnp.float32)).astype(jnp.bfloat16)


def collect(rows, halo_blocks, x_ref, *refs):
    halo_ref, taps_ref = refs[-2:]
    near, far, tiles = x_ref.shape[:3]
    tiles = tiles - 1
    lane = lax.broadcasted_iota(jnp.int32, (far * SUBS, LANES), 1)
    own_tiles = rows * near // LANES
    held = [jnp.zeros((far * SUBS, LANES), jnp.float32) for _ in range(own_tiles)]
    for piece in range(near):
        tile, offset = divmod(rows * piece, LANES)
        value = x_ref[piece, :, tiles, :, :].reshape(far * SUBS, LANES)
        turned = pltpu.roll(value, offset, axis=1) if offset else value
        if offset + rows <= LANES:
            held[tile] = held[tile] + turned
        else:
            held[tile] = held[tile] + jnp.where(lane >= offset, turned, 0.0)
            held[tile + 1] = held[tile + 1] + jnp.where(lane < offset, turned, 0.0)
    height = far * SUBS
    halo_rows = halo_blocks * far * tiles * SUBS
    for tile in range(own_tiles):
        taps_ref[tile * height:(tile + 1) * height, :] = held[tile]
        halo_ref[halo_rows + tile * height:halo_rows + (tile + 1) * height, :] = held[tile]
    for block in range(halo_blocks):
        for z in range(far):
            base = (block * far + z) * tiles * SUBS
            halo_ref[base:base + tiles * SUBS, :] = x_ref[near - halo_blocks + block, z, :tiles, :, :].reshape(-1, LANES)


def toeplitz(row):
    wide = jnp.broadcast_to(row, (LANES, row.shape[1]))
    return pltpu.roll(wide, 0, axis=1, stride=1, stride_axis=0)[:, LANES:]


def shifted(value, steps):
    if steps == 0:
        return value
    blank = jnp.zeros((steps, value.shape[1]), value.dtype)
    return jnp.concatenate([value[steps:], blank], axis=0)


def lay_rows(row_ref, pieces, count, height, rows_of):
    per = (row_ref.shape[0] - 2) // count
    row_ref[0] = jnp.zeros(row_ref.shape[1:], jnp.float32)
    row_ref[row_ref.shape[0] - 1] = jnp.zeros(row_ref.shape[1:], jnp.float32)
    me = lax.axis_index("far")
    for back, (ref, base) in enumerate(pieces):
        source = lax.rem(me + count - back, count)
        for tile in range(per):
            row_ref[1 + source * per + tile] = rows_of(ref, base + tile * height)


def row_of(row_ref, chan):
    return jnp.concatenate([row_ref[t, pl.ds(chan, 1), :] for t in range(row_ref.shape[0])], axis=1)


def forward(halo_blocks, tiles, x_ref, halo_ref, *refs):
    others, (y_ref, row_ref, held_ref) = refs[:-3], refs[-3:]
    far = len(others) + 1
    chans = far * SUBS
    near = y_ref.shape[0] // (far * tiles * SUBS)
    chunk = far * (tiles + 1) * SUBS
    halo_rows = halo_blocks * far * tiles * SUBS
    pieces = [(others[0], 0), (halo_ref, halo_rows)] + [(ref, 0) for ref in others[1:]]
    lay_rows(row_ref, pieces, far, chans, lambda ref, base: ref[base:base + chans, :])
    first = lax.axis_index("far") == 0
    for block in range(halo_blocks):
        for z in range(far):
            source = (block * far + z) * tiles * SUBS
            target = block * chunk + z * (tiles + 1) * SUBS
            value = halo_ref[source:source + tiles * SUBS, :]
            held_ref[target:target + tiles * SUBS, :] = jnp.where(first, 0.0, value)
    held_ref[halo_blocks * chunk:, :] = x_ref[...]
    depth = row_ref.shape[0] - 1

    def one(chan, carry):
        z, i = lax.div(chan, SUBS), lax.rem(chan, SUBS)
        high_t, low_t = split(toeplitz(row_of(row_ref, chan)))
        moved = {}
        for k in range(tiles):
            for steps in range(halo_blocks + 1):
                start = (halo_blocks - steps) * chunk + z * (tiles + 1) * SUBS + k * SUBS + i
                moved[k, steps] = jnp.concatenate(split(held_ref[pl.ds(start, near, stride=chunk), :]), axis=0)
        columns = []
        for d in range(depth):
            parts = []
            for k in range(tiles):
                turns, at = divmod(k - d, tiles)
                parts.append(moved[at, -turns])
            columns.append(jnp.concatenate(parts, axis=0))
        left = jnp.concatenate(columns, axis=1)
        right = jnp.concatenate(
            [jnp.concatenate([t[:, d * LANES:(d + 1) * LANES] for t in (high_t, low_t)], axis=1) for d in range(depth)],
            axis=0,
        )
        total = jnp.dot(left, right, preferred_element_type=jnp.float32)
        total = total[:, :LANES] + total[:, LANES:]
        for k in range(tiles):
            base = 2 * near * k
            value = total[base:base + near] + total[base + near:base + 2 * near]
            y_ref[pl.ds((z * tiles + k) * SUBS + i, near, stride=far * tiles * SUBS), :] = value
        return carry

    lax.fori_loop(0, chans, one, 0, unroll=8)


def gradient(near, tiles, halo_rows, g_ref, halo_ref, *refs):
    others, (out_ref, token_ref, row_ref, held_ref) = refs[:-4], refs[-4:]
    token_ref[...] = jnp.zeros(token_ref.shape, jnp.float32)
    far = len(others) + 1
    me = lax.axis_index("far")
    pieces = [(others[0], 0), (halo_ref, halo_rows)] + [(ref, 0) for ref in others[1:]]
    lay_rows(row_ref, pieces, far, far * SUBS,
             lambda ref, base: ref[pl.ds(pl.multiple_of(base + me * SUBS, SUBS), SUBS), :])
    depth = row_ref.shape[0] - 1
    chunk = tiles * SUBS
    blocks = near * far

    def one(chan, carry):
        high_t, low_t = split(toeplitz(row_of(row_ref, chan)))
        moved = {}
        for k in range(tiles):
            value = jnp.concatenate(
                [g_ref[pl.ds((z * tiles + k) * SUBS + chan, near, stride=far * chunk), :] for z in range(far)], axis=0)
            for steps in range((depth + tiles - 2) // tiles + 1):
                moved[k, steps] = jnp.concatenate(split(shifted(value, steps)), axis=0)
        columns = []
        for d in range(depth):
            parts = []
            for k in range(tiles):
                turns, at = divmod(k + d, tiles)
                parts.append(moved[at, turns])
            columns.append(jnp.concatenate(parts, axis=0))
        left = jnp.concatenate(columns, axis=1)
        right = jnp.concatenate([high_t, low_t], axis=0)
        total = lax.dot_general(left, right, (((1,), (1,)), ((), ())), preferred_element_type=jnp.float32)
        total = total[:, :LANES] + total[:, LANES:]
        for k in range(tiles):
            base = 2 * blocks * k
            value = total[base:base + blocks] + total[base + blocks:base + 2 * blocks]
            held_ref[pl.ds(k * SUBS + chan, blocks, stride=chunk), :] = value
        return carry

    lax.fori_loop(0, SUBS, one, 0, unroll=2)
    for tile in range(blocks * tiles):
        out_ref[:, tile * LANES:(tile + 1) * LANES] = held_ref[tile * SUBS:(tile + 1) * SUBS, :]


def call(body, shapes, scratch=(), flops=0, moved=0, operands=0, after=0, room=40):
    specs = [pl.BlockSpec(memory_space=pltpu.VMEM)] * operands + [pl.BlockSpec(memory_space=pl.ANY)] * after
    shapes = [jax.ShapeDtypeStruct(shape, jnp.float32) for shape in shapes]
    return pl.pallas_call(
        body,
        out_shape=shapes if len(shapes) > 1 else shapes[0],
        **({"in_specs": specs} if specs else {}),
        scratch_shapes=list(scratch),
        compiler_params=pltpu.CompilerParams(vmem_limit_bytes=room * 1024 * 1024),
        cost_estimate=pl.CostEstimate(flops=flops, bytes_accessed=moved, transcendentals=0),
    )


def local(inputs, cotangent, filter_rows, skip_gain, band_blocks):
    far = lax.axis_size("far")
    near = lax.axis_size("near")
    count = far * near
    block_len, chans = inputs.shape
    rows = filter_rows.shape[0]
    tiles = block_len // LANES
    lag_tiles = rows * count // LANES
    halo_blocks = rows * count // block_len
    size = block_len * chans * 4

    def exchanged(value, axes):
        return lax.all_to_all(value, axes, split_axis=0, concat_axis=0, tiled=True)

    def ahead(value, steps):
        return lax.ppermute(value, "far", [(z, (z + steps) % far) for z in range(far)])

    sent_g = call(pack_by_far, [(near, tiles, SUBS, LANES)] * far,
                  [pltpu.VMEM((far, near, tiles, SUBS, LANES), jnp.float32)], moved=2 * size)(cotangent)
    parts = [ahead(part, steps) if steps else part for steps, part in enumerate(sent_g)]
    stacked = call(stack, [(near, far, tiles, SUBS, LANES)], flops=1 * 10 ** 10, moved=2 * size)(*parts)
    got_g = exchanged(stacked, "near").reshape(-1, LANES)
    sent_x = call(pack_with_taps, [(near, far, tiles + 1, SUBS, LANES)], moved=2 * size, room=60)(
        inputs, filter_rows, skip_gain[None, :], band_blocks[None, :])
    got_x = exchanged(sent_x, "near")
    halo_rows = halo_blocks * far * tiles * SUBS
    own_taps = lag_tiles // far * far * SUBS
    halo, taps = call(lambda *refs: collect(rows, halo_blocks, *refs),
                      [(halo_rows + own_taps, LANES), (own_taps, LANES)], moved=size, operands=1, after=1)(got_x, stacked)
    got_halo = ahead(halo, 1)
    pieces = [taps] + [ahead(taps, steps) for steps in range(2, far)]
    def row(height):
        return pltpu.VMEM((lag_tiles + 2, height, LANES), jnp.float32)

    got_x = got_x.reshape(-1, LANES)
    held_rows = (near + halo_blocks) * far * (tiles + 1) * SUBS
    flops = 2 * far * SUBS * 2 * near * tiles * (lag_tiles + 1) * LANES * 2 * LANES
    sent_y = call(lambda *refs: forward(halo_blocks, tiles, *refs), [(count * tiles * SUBS, LANES)],
                  [row(far * SUBS), pltpu.VMEM((held_rows, LANES), jnp.float32)], 40 * flops, 2 * size)(
        got_x, got_halo, *pieces)
    got_y = exchanged(sent_y.reshape(near, far, tiles, SUBS, LANES), "near")
    input_grad, token = call(lambda *refs: gradient(near, tiles, halo_rows, *refs), [(SUBS, count * block_len), (SUBS, LANES)],
                      [row(SUBS), pltpu.VMEM((count * tiles * SUBS, LANES), jnp.float32)], flops, 3 * size)(
        got_g, got_halo, *pieces)
    outputs = call(unpack, [(block_len, chans)], moved=2 * size, operands=1, after=1)(got_y, token)
    return outputs, input_grad


def solution(mesh):
    count, width = mesh.devices.shape
    fine = Mesh(mesh.devices.reshape(count // NEAR, NEAR, width), ("far", "near", "ch"))
    tokens = ("far", "near")
    return jax.shard_map(
        local,
        mesh=fine,
        in_specs=(P(tokens, "ch"), P(tokens, "ch"), P(tokens, "ch"), P("ch"), P("ch")),
        out_specs=(P(tokens, "ch"), P(("ch", "far", "near"), None)),
        check_vma=False,
    )
```

```python
import jax
import jax.numpy as jnp
from jax import lax
from jax.experimental import pallas as pl
from jax.experimental.pallas import tpu as pltpu
from jax.sharding import Mesh, PartitionSpec as P

LANES = 128
SUBS = 8
NEAR = 8


def store_parts(out_ref, k, part):
    far = out_ref.shape[1]
    step = part.shape[0] // far
    for z in range(far):
        out_ref[:, z, k, :, :] = part[z * step:(z + 1) * step].reshape(-1, SUBS, LANES)


def pack_with_taps(x_ref, taps_ref, gain_ref, band_ref, *refs):
    outs, held_ref = refs[:-1], refs[-1]
    block_len = x_ref.shape[0]
    tiles = block_len // LANES
    for k in range(tiles):
        store_parts(held_ref, k, x_ref[k * LANES:(k + 1) * LANES, :].T)
    rows, chans = taps_ref.shape
    place = lax.axis_index("far") * NEAR + lax.axis_index("near")
    lag = place * rows + lax.broadcasted_iota(jnp.int32, (rows, chans), 0)
    kept = jnp.where(lag < band_ref[...] * block_len, taps_ref[...], 0.0)
    kept = kept + jnp.where(lag == 0, gain_ref[...], 0.0)
    kept = jnp.concatenate([kept, jnp.zeros((LANES - rows, chans), jnp.float32)], axis=0)
    store_parts(held_ref, tiles, kept.T)
    for bits, out_ref in enumerate(outs):
        out_ref[...] = held_ref[other(bits)]


def other(bits):
    return lax.axis_index("near") ^ bits


def merge(parts, held_ref):
    for bits, ref in enumerate(parts):
        held_ref[other(bits)] = ref[...]


def pack_plain(x_ref, out_ref):
    for k in range(x_ref.shape[0] // LANES):
        part = x_ref[k * LANES:(k + 1) * LANES, :].T
        out_ref[:, k, :, :] = part.reshape(-1, SUBS, LANES)


def unpack(*refs):
    parts, (out_ref, held_ref) = refs[:-2], refs[-2:]
    merge(parts, held_ref)
    for k in range(out_ref.shape[0] // LANES):
        part = jnp.concatenate([held_ref[:, z, k, :, :].reshape(-1, LANES) for z in range(held_ref.shape[1])], axis=0)
        out_ref[k * LANES:(k + 1) * LANES, :] = part.T


def split(value):
    high = value.astype(jnp.bfloat16)
    return high, (value - high.astype(jnp.float32)).astype(jnp.bfloat16)


def collect(rows, halo_blocks, *refs):
    parts, (halo_ref, taps_ref, x_ref) = refs[:-3], refs[-3:]
    merge(parts, x_ref)
    near, far, tiles = x_ref.shape[:3]
    tiles = tiles - 1
    lane = lax.broadcasted_iota(jnp.int32, (far * SUBS, LANES), 1)
    own_tiles = rows * near // LANES
    held = [jnp.zeros((far * SUBS, LANES), jnp.float32) for _ in range(own_tiles)]
    for piece in range(near):
        tile, offset = divmod(rows * piece, LANES)
        value = x_ref[piece, :, tiles, :, :].reshape(far * SUBS, LANES)
        turned = pltpu.roll(value, offset, axis=1) if offset else value
        if offset + rows <= LANES:
            held[tile] = held[tile] + turned
        else:
            held[tile] = held[tile] + jnp.where(lane >= offset, turned, 0.0)
            held[tile + 1] = held[tile + 1] + jnp.where(lane < offset, turned, 0.0)
    height = far * SUBS
    halo_rows = halo_blocks * far * tiles * SUBS
    for tile in range(own_tiles):
        taps_ref[tile * height:(tile + 1) * height, :] = held[tile]
        halo_ref[halo_rows + tile * height:halo_rows + (tile + 1) * height, :] = held[tile]
    for block in range(halo_blocks):
        for z in range(far):
            base = (block * far + z) * tiles * SUBS
            halo_ref[base:base + tiles * SUBS, :] = x_ref[near - halo_blocks + block, z, :tiles, :, :].reshape(-1, LANES)


def toeplitz(row):
    wide = jnp.broadcast_to(row, (LANES, row.shape[1]))
    return pltpu.roll(wide, 0, axis=1, stride=1, stride_axis=0)[:, LANES:]


def shifted(value, steps):
    if steps == 0:
        return value
    blank = jnp.zeros((steps, value.shape[1]), value.dtype)
    return jnp.concatenate([value[steps:], blank], axis=0)


def lay_rows(row_ref, pieces, count, height, rows_of):
    per = (row_ref.shape[0] - 2) // count
    row_ref[0] = jnp.zeros(row_ref.shape[1:], jnp.float32)
    row_ref[row_ref.shape[0] - 1] = jnp.zeros(row_ref.shape[1:], jnp.float32)
    me = lax.axis_index("far")
    for back, (ref, base) in enumerate(pieces):
        source = lax.rem(me + count - back, count)
        for tile in range(per):
            row_ref[1 + source * per + tile] = rows_of(ref, base + tile * height)


def row_of(row_ref, chan):
    return jnp.concatenate([row_ref[t, pl.ds(chan, 1), :] for t in range(row_ref.shape[0])], axis=1)


def forward(halo_blocks, tiles, near, far, *refs):
    parts, halo_ref, others, outs = refs[:near], refs[near], refs[near + 1:near + far], refs[near + far:-3]
    y_ref, row_ref, held_ref = refs[-3:]
    chans = far * SUBS
    chunk = far * (tiles + 1) * SUBS
    halo_rows = halo_blocks * far * tiles * SUBS
    pieces = [(others[0], 0), (halo_ref, halo_rows)] + [(ref, 0) for ref in others[1:]]
    lay_rows(row_ref, pieces, far, chans, lambda ref, base: ref[base:base + chans, :])
    first = lax.axis_index("far") == 0
    for block in range(halo_blocks):
        for z in range(far):
            source = (block * far + z) * tiles * SUBS
            target = block * chunk + z * (tiles + 1) * SUBS
            value = halo_ref[source:source + tiles * SUBS, :]
            held_ref[target:target + tiles * SUBS, :] = jnp.where(first, 0.0, value)
    for bits, ref in enumerate(parts):
        at = pl.multiple_of((halo_blocks + other(bits)) * chunk, SUBS)
        held_ref[pl.ds(at, chunk), :] = ref[...].reshape(chunk, LANES)
    depth = row_ref.shape[0] - 1

    def one(chan, carry):
        z, i = lax.div(chan, SUBS), lax.rem(chan, SUBS)
        high_t, low_t = split(toeplitz(row_of(row_ref, chan)))
        moved = {}
        for k in range(tiles):
            for steps in range(halo_blocks + 1):
                start = (halo_blocks - steps) * chunk + z * (tiles + 1) * SUBS + k * SUBS + i
                moved[k, steps] = jnp.concatenate(split(held_ref[pl.ds(start, near, stride=chunk), :]), axis=0)
        columns = []
        for d in range(depth):
            parts = []
            for k in range(tiles):
                turns, at = divmod(k - d, tiles)
                parts.append(moved[at, -turns])
            columns.append(jnp.concatenate(parts, axis=0))
        left = jnp.concatenate(columns, axis=1)
        right = jnp.concatenate(
            [jnp.concatenate([t[:, d * LANES:(d + 1) * LANES] for t in (high_t, low_t)], axis=1) for d in range(depth)],
            axis=0,
        )
        total = jnp.dot(left, right, preferred_element_type=jnp.float32)
        total = total[:, :LANES] + total[:, LANES:]
        for k in range(tiles):
            base = 2 * near * k
            value = total[base:base + near] + total[base + near:base + 2 * near]
            y_ref[pl.ds((z * tiles + k) * SUBS + i, near, stride=far * tiles * SUBS), :] = value
        return carry

    lax.fori_loop(0, chans, one, 0, unroll=8)
    share = far * tiles * SUBS
    for bits, ref in enumerate(outs):
        at = pl.multiple_of(other(bits) * share, SUBS)
        ref[...] = y_ref[pl.ds(at, share), :].reshape(ref.shape)


def gradient(blocks, tiles, halo_rows, g_ref, halo_ref, *refs):
    others, (out_ref, row_ref, held_ref) = refs[:-3], refs[-3:]
    far = len(others) + 1
    me = lax.axis_index("far")
    pieces = [(others[0], 0), (halo_ref, halo_rows)] + [(ref, 0) for ref in others[1:]]
    lay_rows(row_ref, pieces, far, far * SUBS,
             lambda ref, base: ref[pl.ds(pl.multiple_of(base + me * SUBS, SUBS), SUBS), :])
    depth = row_ref.shape[0] - 1
    chunk = tiles * SUBS

    def one(chan, carry):
        high_t, low_t = split(toeplitz(row_of(row_ref, chan)))
        moved = {}
        for k in range(tiles):
            value = g_ref[pl.ds(k * SUBS + chan, blocks, stride=chunk), :]
            for steps in range((depth + tiles - 2) // tiles + 1):
                moved[k, steps] = jnp.concatenate(split(shifted(value, steps)), axis=0)
        columns = []
        for d in range(depth):
            parts = []
            for k in range(tiles):
                turns, at = divmod(k + d, tiles)
                parts.append(moved[at, turns])
            columns.append(jnp.concatenate(parts, axis=0))
        left = jnp.concatenate(columns, axis=1)
        right = jnp.concatenate([high_t, low_t], axis=0)
        total = lax.dot_general(left, right, (((1,), (1,)), ((), ())), preferred_element_type=jnp.float32)
        total = total[:, :LANES] + total[:, LANES:]
        for k in range(tiles):
            base = 2 * blocks * k
            value = total[base:base + blocks] + total[base + blocks:base + 2 * blocks]
            held_ref[pl.ds(k * SUBS + chan, blocks, stride=chunk), :] = value
        return carry

    lax.fori_loop(0, SUBS, one, 0, unroll=2)
    for tile in range(blocks * tiles):
        out_ref[:, tile * LANES:(tile + 1) * LANES] = held_ref[tile * SUBS:(tile + 1) * SUBS, :]


def call(body, shapes, scratch=(), flops=0, moved=0, operands=0, after=0, room=40):
    specs = [pl.BlockSpec(memory_space=pltpu.VMEM)] * operands + [pl.BlockSpec(memory_space=pl.ANY)] * after
    shapes = [jax.ShapeDtypeStruct(shape, jnp.float32) for shape in shapes]
    return pl.pallas_call(
        body,
        out_shape=shapes if len(shapes) > 1 else shapes[0],
        **({"in_specs": specs} if specs else {}),
        scratch_shapes=list(scratch),
        compiler_params=pltpu.CompilerParams(vmem_limit_bytes=room * 1024 * 1024),
        cost_estimate=pl.CostEstimate(flops=flops, bytes_accessed=moved, transcendentals=0),
    )


def local(inputs, cotangent, filter_rows, skip_gain, band_blocks):
    far = lax.axis_size("far")
    near = lax.axis_size("near")
    count = far * near
    block_len, chans = inputs.shape
    rows = filter_rows.shape[0]
    tiles = block_len // LANES
    lag_tiles = rows * count // LANES
    halo_blocks = rows * count // block_len
    size = block_len * chans * 4

    def ahead(value, steps):
        return lax.ppermute(value, "far", [(z, (z + steps) % far) for z in range(far)])

    def swapped(parts):
        pairs = [[(n, n ^ bits) for n in range(near)] for bits in range(near)]
        return [lax.ppermute(part, "near", pairs[bits]) if bits else part for bits, part in enumerate(parts)]

    share = (far, tiles + 1, SUBS, LANES)
    got_x = swapped(call(pack_with_taps, [share] * near, [pltpu.VMEM((near, *share), jnp.float32)], moved=2 * size, room=60)(
        inputs, filter_rows, skip_gain[None, :], band_blocks[None, :]))
    halo_rows = halo_blocks * far * tiles * SUBS
    own_taps = lag_tiles // far * far * SUBS
    halo, taps = call(lambda *refs: collect(rows, halo_blocks, *refs), [(halo_rows + own_taps, LANES), (own_taps, LANES)],
                      [pltpu.VMEM((near, *share), jnp.float32)], moved=size)(*got_x)
    got_halo = ahead(halo, 1)
    pieces = [taps] + [ahead(taps, steps) for steps in range(2, far)]

    sent_g = call(pack_plain, [(count, tiles, SUBS, LANES)], moved=2 * size)(cotangent)
    got_g = lax.all_to_all(sent_g, ("far", "near"), split_axis=0, concat_axis=0, tiled=True).reshape(-1, LANES)

    def row(height):
        return pltpu.VMEM((lag_tiles + 2, height, LANES), jnp.float32)

    all_rows = pltpu.VMEM((count * tiles * SUBS, LANES), jnp.float32)
    held_rows = (near + halo_blocks) * far * (tiles + 1) * SUBS
    flops = 2 * far * SUBS * 2 * near * tiles * (lag_tiles + 1) * LANES * 2 * LANES
    share = (far, tiles, SUBS, LANES)
    got_y = swapped(call(lambda *refs: forward(halo_blocks, tiles, near, far, *refs), [share] * near,
                         [all_rows, row(far * SUBS), pltpu.VMEM((held_rows, LANES), jnp.float32)], 40 * flops, 2 * size)(
        *got_x, got_halo, *pieces))
    input_grad = call(lambda *refs: gradient(count, tiles, halo_rows, *refs), [(SUBS, count * block_len)],
                      [row(SUBS), all_rows], flops, 3 * size)(got_g, got_halo, *pieces)
    outputs = call(unpack, [(block_len, chans)], [pltpu.VMEM((near, *share), jnp.float32)], moved=2 * size)(*got_y)
    return outputs, input_grad


def solution(mesh):
    count, width = mesh.devices.shape
    fine = Mesh(mesh.devices.reshape(count // NEAR, NEAR, width), ("far", "near", "ch"))
    tokens = ("far", "near")
    return jax.shard_map(
        local,
        mesh=fine,
        in_specs=(P(tokens, "ch"), P(tokens, "ch"), P(tokens, "ch"), P("ch"), P("ch")),
        out_specs=(P(tokens, "ch"), P(("ch", "far", "near"), None)),
        check_vma=False,
    )
```

```python
import jax
import jax.numpy as jnp
from jax import lax
from jax.experimental import pallas as pl
from jax.experimental.pallas import tpu as pltpu
from jax.sharding import Mesh, PartitionSpec as P

LANES = 128
SUBS = 8
NEAR = 8
ORDER = (0, 4, 5, 2, 6, 3, 7, 1)


def pack_with_taps(x_ref, taps_ref, gain_ref, band_ref, *refs):
    outs, held_ref = refs[:-1], refs[-1]
    block_len, chans = x_ref.shape
    tiles = block_len // LANES
    far = chans // (NEAR * SUBS)
    step = NEAR * SUBS
    for k in range(tiles):
        part = x_ref[k * LANES:(k + 1) * LANES, :].T
        for z in range(far):
            held_ref[:, z * tiles + k, :, :] = part[z * step:(z + 1) * step].reshape(-1, SUBS, LANES)
    rows = taps_ref.shape[0]
    place = lax.axis_index("far") * NEAR + lax.axis_index("near")
    lag = place * rows + lax.broadcasted_iota(jnp.int32, (rows, chans), 0)
    kept = jnp.where(lag < band_ref[...] * block_len, taps_ref[...], 0.0)
    kept = kept + jnp.where(lag == 0, gain_ref[...], 0.0)
    kept = jnp.concatenate([kept, jnp.zeros((LANES - rows, chans), jnp.float32)], axis=0).T
    for pair in range(far // 2):
        low, high = (kept[z * step:(z + 1) * step] for z in (2 * pair, 2 * pair + 1))
        both = low + pltpu.roll(high, LANES // 2, axis=1)
        held_ref[:, far * tiles + pair, :, :] = both.reshape(-1, SUBS, LANES)
    for bits, out_ref in zip(ORDER, outs):
        out_ref[...] = held_ref[other(bits)]


def other(bits):
    return lax.axis_index("near") ^ bits


def merge(parts, held_ref):
    for bits, ref in zip(ORDER, parts):
        held_ref[other(bits)] = ref[...]


def pack_plain(g_ref, own_ref, out_ref, same_ref):
    for k in range(g_ref.shape[0] // LANES):
        part = g_ref[k * LANES:(k + 1) * LANES, :].T
        out_ref[:, k, :, :] = part.reshape(-1, SUBS, LANES)
    same_ref[...] = own_ref[...]


def unpack(*refs):
    parts, (out_ref, held_ref) = refs[:NEAR], refs[-2:]
    merge(parts, held_ref)
    tiles = out_ref.shape[0] // LANES
    for k in range(tiles):
        picked = [held_ref[:, at, :, :].reshape(-1, LANES) for at in range(k, held_ref.shape[1], tiles)]
        out_ref[k * LANES:(k + 1) * LANES, :] = jnp.concatenate(picked, axis=0).T


def split(value):
    high = value.astype(jnp.bfloat16)
    return high, (value - high.astype(jnp.float32)).astype(jnp.bfloat16)


def collect(rows, halo_blocks, tiles, *refs):
    parts, (halo_ref, taps_ref, x_ref) = refs[:-3], refs[-3:]
    merge(parts, x_ref)
    near = len(parts)
    x_tiles = x_ref.shape[1] * 2 * tiles // (2 * tiles + 1)
    far = x_tiles // tiles
    height = far * SUBS
    lane = lax.broadcasted_iota(jnp.int32, (height, LANES), 1)
    own_tiles = rows * near // LANES
    held = [jnp.zeros((height, LANES), jnp.float32) for _ in range(own_tiles)]
    for piece in range(near):
        tile, offset = divmod(rows * piece, LANES)
        values = []
        for pair in range(far // 2):
            both = x_ref[piece, x_tiles + pair]
            values += [both, pltpu.roll(both, LANES // 2, axis=1)]
        value = jnp.concatenate(values, axis=0)
        turned = pltpu.roll(value, offset, axis=1) if offset else value
        held[tile] = held[tile] + jnp.where((lane >= offset) & (lane < offset + rows), turned, 0.0)
        if offset + rows > LANES:
            held[tile + 1] = held[tile + 1] + jnp.where(lane < offset + rows - LANES, turned, 0.0)
    share = x_tiles * SUBS
    halo_rows = halo_blocks * share
    for tile in range(own_tiles):
        taps_ref[tile * height:(tile + 1) * height, :] = held[tile]
        halo_ref[halo_rows + tile * height:halo_rows + (tile + 1) * height, :] = held[tile]
    for block in range(halo_blocks):
        halo_ref[block * share:(block + 1) * share, :] = x_ref[near - halo_blocks + block, :x_tiles].reshape(share, LANES)


def toeplitz(row):
    wide = jnp.broadcast_to(row, (LANES, row.shape[1]))
    return pltpu.roll(wide, 0, axis=1, stride=1, stride_axis=0)[:, LANES:]


def shifted(value, steps):
    if steps == 0:
        return value
    blank = jnp.zeros((steps, value.shape[1]), value.dtype)
    return jnp.concatenate([value[steps:], blank], axis=0)


def lay_rows(row_ref, pieces, count, height, rows_of):
    per = (row_ref.shape[0] - 2) // count
    row_ref[0] = jnp.zeros(row_ref.shape[1:], jnp.float32)
    row_ref[row_ref.shape[0] - 1] = jnp.zeros(row_ref.shape[1:], jnp.float32)
    me = lax.axis_index("far")
    for back, (ref, base) in enumerate(pieces):
        source = lax.rem(me + count - back, count)
        for tile in range(per):
            row_ref[1 + source * per + tile] = rows_of(ref, base + tile * height)


def row_of(row_ref, chan):
    return jnp.concatenate([row_ref[t, pl.ds(chan, 1), :] for t in range(row_ref.shape[0])], axis=1)


def forward(halo_blocks, tiles, near, far, *refs):
    parts, halo_ref, others, outs = refs[:near], refs[near], refs[near + 1:near + far], refs[near + far:-3]
    y_ref, row_ref, held_ref = refs[-3:]
    chans = far * SUBS
    chunk = parts[0].shape[0] * SUBS
    halo_rows = halo_blocks * far * tiles * SUBS
    pieces = [(others[0], 0), (halo_ref, halo_rows)] + [(ref, 0) for ref in others[1:]]
    lay_rows(row_ref, pieces, far, chans, lambda ref, base: ref[base:base + chans, :])
    first = lax.axis_index("far") == 0
    share = far * tiles * SUBS
    for block in range(halo_blocks):
        value = halo_ref[block * share:(block + 1) * share, :]
        held_ref[block * chunk:block * chunk + share, :] = jnp.where(first, 0.0, value)
    for bits, ref in zip(ORDER, parts):
        at = pl.multiple_of((halo_blocks + other(bits)) * chunk, SUBS)
        held_ref[pl.ds(at, chunk), :] = ref[...].reshape(chunk, LANES)
    depth = row_ref.shape[0] - 1

    def one(chan, carry):
        z, i = lax.div(chan, SUBS), lax.rem(chan, SUBS)
        high_t, low_t = split(toeplitz(row_of(row_ref, chan)))
        moved = {}
        for k in range(tiles):
            for steps in range(halo_blocks + 1):
                start = (halo_blocks - steps) * chunk + (z * tiles + k) * SUBS + i
                moved[k, steps] = jnp.concatenate(split(held_ref[pl.ds(start, near, stride=chunk), :]), axis=0)
        columns = []
        for d in range(depth):
            parts = []
            for k in range(tiles):
                turns, at = divmod(k - d, tiles)
                parts.append(moved[at, -turns])
            columns.append(jnp.concatenate(parts, axis=0))
        left = jnp.concatenate(columns, axis=1)
        right = jnp.concatenate(
            [jnp.concatenate([t[:, d * LANES:(d + 1) * LANES] for t in (high_t, low_t)], axis=1) for d in range(depth)],
            axis=0,
        )
        total = jnp.dot(left, right, preferred_element_type=jnp.float32)
        total = total[:, :LANES] + total[:, LANES:]
        for k in range(tiles):
            base = 2 * near * k
            value = total[base:base + near] + total[base + near:base + 2 * near]
            y_ref[pl.ds((z * tiles + k) * SUBS + i, near, stride=far * tiles * SUBS), :] = value
        return carry

    lax.fori_loop(0, chans, one, 0, unroll=8)
    for bits, ref in zip(ORDER, outs):
        at = pl.multiple_of(other(bits) * share, SUBS)
        ref[...] = y_ref[pl.ds(at, share), :].reshape(ref.shape)


def gradient(blocks, tiles, halo_rows, g_ref, halo_ref, *refs):
    others, (out_ref, token_ref, row_ref, held_ref) = refs[:-4], refs[-4:]
    token_ref[...] = jnp.zeros(token_ref.shape, jnp.float32)
    far = len(others) + 1
    me = lax.axis_index("far")
    pieces = [(others[0], 0), (halo_ref, halo_rows)] + [(ref, 0) for ref in others[1:]]
    lay_rows(row_ref, pieces, far, far * SUBS,
             lambda ref, base: ref[pl.ds(pl.multiple_of(base + me * SUBS, SUBS), SUBS), :])
    depth = row_ref.shape[0] - 1
    chunk = tiles * SUBS

    def one(chan, carry):
        high_t, low_t = split(toeplitz(row_of(row_ref, chan)))
        moved = {}
        for k in range(tiles):
            value = g_ref[pl.ds(k * SUBS + chan, blocks, stride=chunk), :]
            for steps in range((depth + tiles - 2) // tiles + 1):
                moved[k, steps] = jnp.concatenate(split(shifted(value, steps)), axis=0)
        columns = []
        for d in range(depth):
            parts = []
            for k in range(tiles):
                turns, at = divmod(k + d, tiles)
                parts.append(moved[at, turns])
            columns.append(jnp.concatenate(parts, axis=0))
        left = jnp.concatenate(columns, axis=1)
        right = jnp.concatenate([high_t, low_t], axis=0)
        total = lax.dot_general(left, right, (((1,), (1,)), ((), ())), preferred_element_type=jnp.float32)
        total = total[:, :LANES] + total[:, LANES:]
        for k in range(tiles):
            base = 2 * blocks * k
            value = total[base:base + blocks] + total[base + blocks:base + 2 * blocks]
            held_ref[pl.ds(k * SUBS + chan, blocks, stride=chunk), :] = value
        return carry

    lax.fori_loop(0, SUBS, one, 0, unroll=4)
    for tile in range(blocks * tiles):
        out_ref[:, tile * LANES:(tile + 1) * LANES] = held_ref[tile * SUBS:(tile + 1) * SUBS, :]


def call(body, shapes, scratch=(), flops=0, moved=0, operands=0, after=0, room=40):
    specs = [pl.BlockSpec(memory_space=pltpu.VMEM)] * operands + [pl.BlockSpec(memory_space=pl.ANY)] * after
    shapes = [jax.ShapeDtypeStruct(shape, jnp.float32) for shape in shapes]
    return pl.pallas_call(
        body,
        out_shape=shapes if len(shapes) > 1 else shapes[0],
        **({"in_specs": specs} if specs else {}),
        scratch_shapes=list(scratch),
        compiler_params=pltpu.CompilerParams(vmem_limit_bytes=room * 1024 * 1024),
        cost_estimate=pl.CostEstimate(flops=flops, bytes_accessed=moved, transcendentals=0),
    )


def local(inputs, cotangent, filter_rows, skip_gain, band_blocks):
    far = lax.axis_size("far")
    near = lax.axis_size("near")
    count = far * near
    block_len, chans = inputs.shape
    rows = filter_rows.shape[0]
    tiles = block_len // LANES
    lag_tiles = rows * count // LANES
    halo_blocks = rows * count // block_len
    size = block_len * chans * 4

    def ahead(value, steps):
        return lax.ppermute(value, "far", [(z, (z + steps) % far) for z in range(far)])

    def swapped(parts):
        pairs = [[(n, n ^ bits) for n in range(near)] for bits in range(near)]
        return [lax.ppermute(part, "near", pairs[bits]) if bits else part for bits, part in zip(ORDER, parts)]

    share = (far * tiles + far // 2, SUBS, LANES)
    sent_x = call(pack_with_taps, [share] * near, [pltpu.VMEM((near, *share), jnp.float32)], moved=2 * size, room=60)(
        inputs, filter_rows, skip_gain[None, :], band_blocks[None, :])
    got_x = swapped(sent_x)
    sent_g, got_x[0] = call(pack_plain, [(count, tiles, SUBS, LANES), share], moved=2 * size)(cotangent, sent_x[0])
    halo_rows = halo_blocks * far * tiles * SUBS
    own_taps = lag_tiles // far * far * SUBS
    halo, taps = call(lambda *refs: collect(rows, halo_blocks, tiles, *refs),
                      [(halo_rows + own_taps, LANES), (own_taps, LANES)],
                      [pltpu.VMEM((near, *share), jnp.float32)], moved=size)(*got_x)
    got_halo = ahead(halo, 1)
    pieces = [taps] + [ahead(taps, steps) for steps in range(2, far)]
    got_g = lax.all_to_all(sent_g, ("far", "near"), split_axis=0, concat_axis=0, tiled=True).reshape(-1, LANES)

    def row(height):
        return pltpu.VMEM((lag_tiles + 2, height, LANES), jnp.float32)

    all_rows = pltpu.VMEM((count * tiles * SUBS, LANES), jnp.float32)
    held_rows = (near + halo_blocks) * share[0] * SUBS
    flops = 2 * far * SUBS * 2 * near * tiles * (lag_tiles + 1) * LANES * 2 * LANES
    share = (far * tiles, SUBS, LANES)
    got_y = swapped(call(lambda *refs: forward(halo_blocks, tiles, near, far, *refs), [share] * near,
                         [all_rows, row(far * SUBS), pltpu.VMEM((held_rows, LANES), jnp.float32)], 40 * flops, 2 * size)(
        *got_x, got_halo, *pieces))
    input_grad, token = call(lambda *refs: gradient(count, tiles, halo_rows, *refs),
                             [(SUBS, count * block_len), (SUBS, LANES)],
                             [row(SUBS), all_rows], flops, 3 * size)(got_g, got_halo, *pieces)
    outputs = call(unpack, [(block_len, chans)], [pltpu.VMEM((near, *share), jnp.float32)], moved=2 * size,
                   operands=near, after=1)(*got_y, token)
    return outputs, input_grad


def solution(mesh):
    count, width = mesh.devices.shape
    fine = Mesh(mesh.devices.reshape(count // NEAR, NEAR, width), ("far", "near", "ch"))
    tokens = ("far", "near")
    return jax.shard_map(
        local,
        mesh=fine,
        in_specs=(P(tokens, "ch"), P(tokens, "ch"), P(tokens, "ch"), P("ch"), P("ch")),
        out_specs=(P(tokens, "ch"), P(("ch", "far", "near"), None)),
        check_vma=False,
    )
```

```python
import jax
import jax.numpy as jnp
from jax import lax
from jax.experimental import pallas as pl
from jax.experimental.pallas import tpu as pltpu
from jax.sharding import Mesh, PartitionSpec as P

LANES = 128
SUBS = 8
NEAR = 8
IN_ORDER = (0, 4, 5, 2, 6, 3, 7, 1)
OUT_ORDER = (0, 1, 4, 2, 6, 5, 3, 7)


def pack_with_taps(x_ref, taps_ref, gain_ref, band_ref, *refs):
    outs, held_ref = refs[:-1], refs[-1]
    block_len, chans = x_ref.shape
    tiles = block_len // LANES
    far = chans // (NEAR * SUBS)
    step = NEAR * SUBS
    for k in range(tiles):
        part = x_ref[k * LANES:(k + 1) * LANES, :].T
        for z in range(far):
            held_ref[:, z * tiles + k, :, :] = part[z * step:(z + 1) * step].reshape(-1, SUBS, LANES)
    rows = taps_ref.shape[0]
    place = lax.axis_index("far") * NEAR + lax.axis_index("near")
    lag = place * rows + lax.broadcasted_iota(jnp.int32, (rows, chans), 0)
    kept = jnp.where(lag < band_ref[...] * block_len, taps_ref[...], 0.0)
    kept = kept + jnp.where(lag == 0, gain_ref[...], 0.0)
    kept = jnp.concatenate([kept, jnp.zeros((LANES - rows, chans), jnp.float32)], axis=0).T
    for pair in range(far // 2):
        low, high = (kept[z * step:(z + 1) * step] for z in (2 * pair, 2 * pair + 1))
        both = low + pltpu.roll(high, LANES // 2, axis=1)
        held_ref[:, far * tiles + pair, :, :] = both.reshape(-1, SUBS, LANES)
    for bits, out_ref in zip(IN_ORDER, outs):
        out_ref[...] = held_ref[other(bits)]


def other(bits):
    return lax.axis_index("near") ^ bits


def merge(order, parts, held_ref):
    for bits, ref in zip(order, parts):
        held_ref[other(bits)] = ref[...]


def pack_plain(g_ref, own_ref, out_ref, same_ref):
    for k in range(g_ref.shape[0] // LANES):
        part = g_ref[k * LANES:(k + 1) * LANES, :].T
        out_ref[:, k, :, :] = part.reshape(-1, SUBS, LANES)
    same_ref[...] = own_ref[...]


def unpack(*refs):
    parts, (out_ref, held_ref) = refs[:NEAR], refs[-2:]
    merge(OUT_ORDER, parts, held_ref)
    tiles = out_ref.shape[0] // LANES
    for k in range(tiles):
        picked = [held_ref[:, at, :, :].reshape(-1, LANES) for at in range(k, held_ref.shape[1], tiles)]
        out_ref[k * LANES:(k + 1) * LANES, :] = jnp.concatenate(picked, axis=0).T


def split(value):
    high = value.astype(jnp.bfloat16)
    return high, (value - high.astype(jnp.float32)).astype(jnp.bfloat16)


def collect(rows, halo_blocks, tiles, *refs):
    parts, (halo_ref, taps_ref, x_ref) = refs[:-3], refs[-3:]
    merge(IN_ORDER, parts, x_ref)
    near = len(parts)
    x_tiles = x_ref.shape[1] * 2 * tiles // (2 * tiles + 1)
    far = x_tiles // tiles
    height = far * SUBS
    lane = lax.broadcasted_iota(jnp.int32, (height, LANES), 1)
    own_tiles = rows * near // LANES
    held = [jnp.zeros((height, LANES), jnp.float32) for _ in range(own_tiles)]
    for piece in range(near):
        tile, offset = divmod(rows * piece, LANES)
        values = []
        for pair in range(far // 2):
            both = x_ref[piece, x_tiles + pair]
            values += [both, pltpu.roll(both, LANES // 2, axis=1)]
        value = jnp.concatenate(values, axis=0)
        turned = pltpu.roll(value, offset, axis=1) if offset else value
        held[tile] = held[tile] + jnp.where((lane >= offset) & (lane < offset + rows), turned, 0.0)
        if offset + rows > LANES:
            held[tile + 1] = held[tile + 1] + jnp.where(lane < offset + rows - LANES, turned, 0.0)
    share = x_tiles * SUBS
    halo_rows = halo_blocks * share
    for tile in range(own_tiles):
        taps_ref[tile * height:(tile + 1) * height, :] = held[tile]
        halo_ref[halo_rows + tile * height:halo_rows + (tile + 1) * height, :] = held[tile]
    for block in range(halo_blocks):
        halo_ref[block * share:(block + 1) * share, :] = x_ref[near - halo_blocks + block, :x_tiles].reshape(share, LANES)


def toeplitz(row):
    wide = jnp.broadcast_to(row, (LANES, row.shape[1]))
    return pltpu.roll(wide, 0, axis=1, stride=1, stride_axis=0)[:, LANES:]


def shifted(value, steps):
    if steps == 0:
        return value
    blank = jnp.zeros((steps, value.shape[1]), value.dtype)
    return jnp.concatenate([value[steps:], blank], axis=0)


def lay_rows(row_ref, pieces, count, height, rows_of):
    per = (row_ref.shape[0] - 2) // count
    row_ref[0] = jnp.zeros(row_ref.shape[1:], jnp.float32)
    row_ref[row_ref.shape[0] - 1] = jnp.zeros(row_ref.shape[1:], jnp.float32)
    me = lax.axis_index("far")
    for back, (ref, base) in enumerate(pieces):
        source = lax.rem(me + count - back, count)
        for tile in range(per):
            row_ref[1 + source * per + tile] = rows_of(ref, base + tile * height)


def row_of(row_ref, chan):
    return jnp.concatenate([row_ref[t, pl.ds(chan, 1), :] for t in range(row_ref.shape[0])], axis=1)


def forward(halo_blocks, tiles, near, far, *refs):
    parts, halo_ref, others, outs = refs[:near], refs[near], refs[near + 1:near + far], refs[near + far:-3]
    y_ref, row_ref, held_ref = refs[-3:]
    chans = far * SUBS
    chunk = parts[0].shape[0] * SUBS
    halo_rows = halo_blocks * far * tiles * SUBS
    pieces = [(others[0], 0), (halo_ref, halo_rows)] + [(ref, 0) for ref in others[1:]]
    lay_rows(row_ref, pieces, far, chans, lambda ref, base: ref[base:base + chans, :])
    first = lax.axis_index("far") == 0
    share = far * tiles * SUBS
    for block in range(halo_blocks):
        value = halo_ref[block * share:(block + 1) * share, :]
        held_ref[block * chunk:block * chunk + share, :] = jnp.where(first, 0.0, value)
    for bits, ref in zip(IN_ORDER, parts):
        at = pl.multiple_of((halo_blocks + other(bits)) * chunk, SUBS)
        held_ref[pl.ds(at, chunk), :] = ref[...].reshape(chunk, LANES)
    depth = row_ref.shape[0] - 1

    def one(chan, carry):
        z, i = lax.div(chan, SUBS), lax.rem(chan, SUBS)
        high_t, low_t = split(toeplitz(row_of(row_ref, chan)))
        moved = {}
        for k in range(tiles):
            for steps in range(halo_blocks + 1):
                start = (halo_blocks - steps) * chunk + (z * tiles + k) * SUBS + i
                moved[k, steps] = jnp.concatenate(split(held_ref[pl.ds(start, near, stride=chunk), :]), axis=0)
        columns = []
        for d in range(depth):
            parts = []
            for k in range(tiles):
                turns, at = divmod(k - d, tiles)
                parts.append(moved[at, -turns])
            columns.append(jnp.concatenate(parts, axis=0))
        left = jnp.concatenate(columns, axis=1)
        right = jnp.concatenate(
            [jnp.concatenate([t[:, d * LANES:(d + 1) * LANES] for t in (high_t, low_t)], axis=1) for d in range(depth)],
            axis=0,
        )
        total = jnp.dot(left, right, preferred_element_type=jnp.float32)
        total = total[:, :LANES] + total[:, LANES:]
        for k in range(tiles):
            base = 2 * near * k
            value = total[base:base + near] + total[base + near:base + 2 * near]
            y_ref[pl.ds((z * tiles + k) * SUBS + i, near, stride=far * tiles * SUBS), :] = value
        return carry

    lax.fori_loop(0, chans, one, 0, unroll=16)
    for bits, ref in zip(OUT_ORDER, outs):
        at = pl.multiple_of(other(bits) * share, SUBS)
        ref[...] = y_ref[pl.ds(at, share), :].reshape(ref.shape)


def gradient(blocks, tiles, halo_rows, g_ref, halo_ref, *refs):
    others, (out_ref, token_ref, row_ref, held_ref) = refs[:-4], refs[-4:]
    token_ref[...] = jnp.zeros(token_ref.shape, jnp.float32)
    far = len(others) + 1
    me = lax.axis_index("far")
    pieces = [(others[0], 0), (halo_ref, halo_rows)] + [(ref, 0) for ref in others[1:]]
    lay_rows(row_ref, pieces, far, far * SUBS,
             lambda ref, base: ref[pl.ds(pl.multiple_of(base + me * SUBS, SUBS), SUBS), :])
    depth = row_ref.shape[0] - 1
    chunk = tiles * SUBS

    def one(chan, carry):
        high_t, low_t = split(toeplitz(row_of(row_ref, chan)))
        moved = {}
        for k in range(tiles):
            value = g_ref[pl.ds(k * SUBS + chan, blocks, stride=chunk), :]
            for steps in range((depth + tiles - 2) // tiles + 1):
                moved[k, steps] = jnp.concatenate(split(shifted(value, steps)), axis=0)
        columns = []
        for d in range(depth):
            parts = []
            for k in range(tiles):
                turns, at = divmod(k + d, tiles)
                parts.append(moved[at, turns])
            columns.append(jnp.concatenate(parts, axis=0))
        left = jnp.concatenate(columns, axis=1)
        right = jnp.concatenate([high_t, low_t], axis=0)
        total = lax.dot_general(left, right, (((1,), (1,)), ((), ())), preferred_element_type=jnp.float32)
        total = total[:, :LANES] + total[:, LANES:]
        for k in range(tiles):
            base = 2 * blocks * k
            value = total[base:base + blocks] + total[base + blocks:base + 2 * blocks]
            held_ref[pl.ds(k * SUBS + chan, blocks, stride=chunk), :] = value
        return carry

    lax.fori_loop(0, SUBS, one, 0, unroll=8)
    for tile in range(blocks * tiles):
        out_ref[:, tile * LANES:(tile + 1) * LANES] = held_ref[tile * SUBS:(tile + 1) * SUBS, :]


def call(body, shapes, scratch=(), flops=0, moved=0, operands=0, after=0, room=40):
    specs = [pl.BlockSpec(memory_space=pltpu.VMEM)] * operands + [pl.BlockSpec(memory_space=pl.ANY)] * after
    shapes = [jax.ShapeDtypeStruct(shape, jnp.float32) for shape in shapes]
    return pl.pallas_call(
        body,
        out_shape=shapes if len(shapes) > 1 else shapes[0],
        **({"in_specs": specs} if specs else {}),
        scratch_shapes=list(scratch),
        compiler_params=pltpu.CompilerParams(vmem_limit_bytes=room * 1024 * 1024),
        cost_estimate=pl.CostEstimate(flops=flops, bytes_accessed=moved, transcendentals=0),
    )


def local(inputs, cotangent, filter_rows, skip_gain, band_blocks):
    far = lax.axis_size("far")
    near = lax.axis_size("near")
    count = far * near
    block_len, chans = inputs.shape
    rows = filter_rows.shape[0]
    tiles = block_len // LANES
    lag_tiles = rows * count // LANES
    halo_blocks = rows * count // block_len
    size = block_len * chans * 4

    def ahead(value, steps):
        return lax.ppermute(value, "far", [(z, (z + steps) % far) for z in range(far)])

    def swapped(parts, order):
        pairs = [[(n, n ^ bits) for n in range(near)] for bits in range(near)]
        return [lax.ppermute(part, "near", pairs[bits]) if bits else part for bits, part in zip(order, parts)]

    share = (far * tiles + far // 2, SUBS, LANES)
    sent_x = call(pack_with_taps, [share] * near, [pltpu.VMEM((near, *share), jnp.float32)], moved=2 * size, room=60)(
        inputs, filter_rows, skip_gain[None, :], band_blocks[None, :])
    got_x = swapped(sent_x, IN_ORDER)
    sent_g, got_x[0] = call(pack_plain, [(count, tiles, SUBS, LANES), share], moved=2 * size)(cotangent, sent_x[0])
    halo_rows = halo_blocks * far * tiles * SUBS
    own_taps = lag_tiles // far * far * SUBS
    halo, taps = call(lambda *refs: collect(rows, halo_blocks, tiles, *refs),
                      [(halo_rows + own_taps, LANES), (own_taps, LANES)],
                      [pltpu.VMEM((near, *share), jnp.float32)], moved=size)(*got_x)
    got_halo = ahead(halo, 1)
    pieces = [taps] + [ahead(taps, steps) for steps in range(2, far)]
    got_g = lax.all_to_all(sent_g, ("far", "near"), split_axis=0, concat_axis=0, tiled=True).reshape(-1, LANES)

    def row(height):
        return pltpu.VMEM((lag_tiles + 2, height, LANES), jnp.float32)

    all_rows = pltpu.VMEM((count * tiles * SUBS, LANES), jnp.float32)
    held_rows = (near + halo_blocks) * share[0] * SUBS
    flops = 2 * far * SUBS * 2 * near * tiles * (lag_tiles + 1) * LANES * 2 * LANES
    share = (far * tiles, SUBS, LANES)
    got_y = swapped(call(lambda *refs: forward(halo_blocks, tiles, near, far, *refs), [share] * near,
                         [all_rows, row(far * SUBS), pltpu.VMEM((held_rows, LANES), jnp.float32)], 40 * flops, 2 * size)(
        *got_x, got_halo, *pieces), OUT_ORDER)
    input_grad, token = call(lambda *refs: gradient(count, tiles, halo_rows, *refs),
                             [(SUBS, count * block_len), (SUBS, LANES)],
                             [row(SUBS), all_rows], flops, 3 * size)(got_g, got_halo, *pieces)
    outputs = call(unpack, [(block_len, chans)], [pltpu.VMEM((near, *share), jnp.float32)], moved=2 * size,
                   operands=near, after=1)(*got_y, token)
    return outputs, input_grad


def solution(mesh):
    count, width = mesh.devices.shape
    fine = Mesh(mesh.devices.reshape(count // NEAR, NEAR, width), ("far", "near", "ch"))
    tokens = ("far", "near")
    return jax.shard_map(
        local,
        mesh=fine,
        in_specs=(P(tokens, "ch"), P(tokens, "ch"), P(tokens, "ch"), P("ch"), P("ch")),
        out_specs=(P(tokens, "ch"), P(("ch", "far", "near"), None)),
        check_vma=False,
    )
```

```python
import jax
import jax.numpy as jnp
from jax import lax
from jax.experimental import pallas as pl
from jax.experimental.pallas import tpu as pltpu
from jax.sharding import Mesh, PartitionSpec as P

LANES = 128
SUBS = 8
NEAR = 8
IN_ORDER = (0, 4, 5, 2, 6, 3, 7, 1)
OUT_ORDER = (0, 1, 4, 2, 6, 5, 3, 7)


def pack_with_taps(x_ref, taps_ref, gain_ref, band_ref, *refs):
    outs, held_ref = refs[:-1], refs[-1]
    block_len, chans = x_ref.shape
    tiles = block_len // LANES
    far = chans // (NEAR * SUBS)
    step = NEAR * SUBS
    for k in range(tiles):
        part = x_ref[k * LANES:(k + 1) * LANES, :].T
        for z in range(far):
            held_ref[:, z * tiles + k, :, :] = part[z * step:(z + 1) * step].reshape(-1, SUBS, LANES)
    rows = taps_ref.shape[0]
    place = lax.axis_index("far") * NEAR + lax.axis_index("near")
    lag = place * rows + lax.broadcasted_iota(jnp.int32, (rows, chans), 0)
    kept = jnp.where(lag < band_ref[...] * block_len, taps_ref[...], 0.0)
    kept = kept + jnp.where(lag == 0, gain_ref[...], 0.0)
    kept = jnp.concatenate([kept, jnp.zeros((LANES - rows, chans), jnp.float32)], axis=0).T
    for pair in range(far // 2):
        low, high = (kept[z * step:(z + 1) * step] for z in (2 * pair, 2 * pair + 1))
        both = low + pltpu.roll(high, LANES // 2, axis=1)
        held_ref[:, far * tiles + pair, :, :] = both.reshape(-1, SUBS, LANES)
    for bits, out_ref in zip(IN_ORDER, outs):
        out_ref[...] = held_ref[other(bits)]


def other(bits):
    return lax.axis_index("near") ^ bits


def merge(order, parts, held_ref):
    for bits, ref in zip(order, parts):
        held_ref[other(bits)] = ref[...]


def pack_plain(g_ref, own_ref, out_ref, same_ref):
    for k in range(g_ref.shape[0] // LANES):
        part = g_ref[k * LANES:(k + 1) * LANES, :].T
        out_ref[:, k, :, :] = part.reshape(-1, SUBS, LANES)
    same_ref[...] = own_ref[...]


def unpack(*refs):
    parts, (out_ref, held_ref) = refs[:NEAR], refs[-2:]
    merge(OUT_ORDER, parts, held_ref)
    tiles = out_ref.shape[0] // LANES
    for k in range(tiles):
        picked = [held_ref[:, at, :, :].reshape(-1, LANES) for at in range(k, held_ref.shape[1], tiles)]
        out_ref[k * LANES:(k + 1) * LANES, :] = jnp.concatenate(picked, axis=0).T


def split(value):
    high = value.astype(jnp.bfloat16)
    return high, (value - high.astype(jnp.float32)).astype(jnp.bfloat16)


def collect(rows, halo_blocks, tiles, *refs):
    parts, (halo_ref, taps_ref, x_ref) = refs[:-3], refs[-3:]
    merge(IN_ORDER, parts, x_ref)
    near = len(parts)
    x_tiles = x_ref.shape[1] * 2 * tiles // (2 * tiles + 1)
    far = x_tiles // tiles
    height = far * SUBS
    lane = lax.broadcasted_iota(jnp.int32, (height, LANES), 1)
    own_tiles = rows * near // LANES
    held = [jnp.zeros((height, LANES), jnp.float32) for _ in range(own_tiles)]
    for piece in range(near):
        tile, offset = divmod(rows * piece, LANES)
        values = []
        for pair in range(far // 2):
            both = x_ref[piece, x_tiles + pair]
            values += [both, pltpu.roll(both, LANES // 2, axis=1)]
        value = jnp.concatenate(values, axis=0)
        turned = pltpu.roll(value, offset, axis=1) if offset else value
        held[tile] = held[tile] + jnp.where((lane >= offset) & (lane < offset + rows), turned, 0.0)
        if offset + rows > LANES:
            held[tile + 1] = held[tile + 1] + jnp.where(lane < offset + rows - LANES, turned, 0.0)
    share = x_tiles * SUBS
    halo_rows = halo_blocks * share
    for tile in range(own_tiles):
        taps_ref[tile * height:(tile + 1) * height, :] = held[tile]
        halo_ref[halo_rows + tile * height:halo_rows + (tile + 1) * height, :] = held[tile]
    for block in range(halo_blocks):
        halo_ref[block * share:(block + 1) * share, :] = x_ref[near - halo_blocks + block, :x_tiles].reshape(share, LANES)


def toeplitz(row):
    wide = jnp.broadcast_to(row, (LANES, row.shape[1]))
    return pltpu.roll(wide, 0, axis=1, stride=1, stride_axis=0)[:, LANES:]


def shifted(value, steps):
    if steps == 0:
        return value
    blank = jnp.zeros((steps, value.shape[1]), value.dtype)
    return jnp.concatenate([value[steps:], blank], axis=0)


def lay_rows(row_ref, pieces, count, height, rows_of):
    per = (row_ref.shape[0] - 2) // count
    row_ref[0] = jnp.zeros(row_ref.shape[1:], jnp.float32)
    row_ref[row_ref.shape[0] - 1] = jnp.zeros(row_ref.shape[1:], jnp.float32)
    me = lax.axis_index("far")
    for back, (ref, base) in enumerate(pieces):
        source = lax.rem(me + count - back, count)
        for tile in range(per):
            row_ref[1 + source * per + tile] = rows_of(ref, base + tile * height)


def row_of(row_ref, chan):
    return jnp.concatenate([row_ref[t, pl.ds(chan, 1), :] for t in range(row_ref.shape[0])], axis=1)


def forward(halo_blocks, tiles, near, far, *refs):
    parts, halo_ref, others, outs = refs[:near], refs[near], refs[near + 1:near + far], refs[near + far:-3]
    y_ref, row_ref, held_ref = refs[-3:]
    chans = far * SUBS
    chunk = parts[0].shape[0] * SUBS
    halo_rows = halo_blocks * far * tiles * SUBS
    pieces = [(others[0], 0), (halo_ref, halo_rows)] + [(ref, 0) for ref in others[1:]]
    lay_rows(row_ref, pieces, far, chans, lambda ref, base: ref[base:base + chans, :])
    first = lax.axis_index("far") == 0
    share = far * tiles * SUBS
    for block in range(halo_blocks):
        value = halo_ref[block * share:(block + 1) * share, :]
        held_ref[block * chunk:block * chunk + share, :] = jnp.where(first, 0.0, value)
    for bits, ref in zip(IN_ORDER, parts):
        at = pl.multiple_of((halo_blocks + other(bits)) * chunk, SUBS)
        held_ref[pl.ds(at, chunk), :] = ref[...].reshape(chunk, LANES)
    depth = row_ref.shape[0] - 1

    def one(chan, carry):
        z, i = lax.div(chan, SUBS), lax.rem(chan, SUBS)
        high_t, low_t = split(toeplitz(row_of(row_ref, chan)))
        moved = {}
        for k in range(tiles):
            for steps in range(halo_blocks + 1):
                start = (halo_blocks - steps) * chunk + (z * tiles + k) * SUBS + i
                moved[k, steps] = jnp.concatenate(split(held_ref[pl.ds(start, near, stride=chunk), :]), axis=0)
        columns = []
        for d in range(depth):
            parts = []
            for k in range(tiles):
                turns, at = divmod(k - d, tiles)
                parts.append(moved[at, -turns])
            columns.append(jnp.concatenate(parts, axis=0))
        left = jnp.concatenate(columns, axis=1)
        right = jnp.concatenate(
            [jnp.concatenate([t[:, d * LANES:(d + 1) * LANES] for t in (high_t, low_t)], axis=1) for d in range(depth)],
            axis=0,
        )
        total = jnp.dot(left, right, preferred_element_type=jnp.float32)
        total = total[:, :LANES] + total[:, LANES:]
        for k in range(tiles):
            base = 2 * near * k
            value = total[base:base + near] + total[base + near:base + 2 * near]
            y_ref[pl.ds((z * tiles + k) * SUBS + i, near, stride=far * tiles * SUBS), :] = value
        return carry

    lax.fori_loop(0, chans, one, 0, unroll=32)
    for bits, ref in zip(OUT_ORDER, outs):
        at = pl.multiple_of(other(bits) * share, SUBS)
        ref[...] = y_ref[pl.ds(at, share), :].reshape(ref.shape)


def gradient(blocks, tiles, halo_rows, g_ref, halo_ref, *refs):
    others, (out_ref, token_ref, row_ref, held_ref) = refs[:-4], refs[-4:]
    token_ref[...] = jnp.zeros(token_ref.shape, jnp.float32)
    far = len(others) + 1
    me = lax.axis_index("far")
    pieces = [(others[0], 0), (halo_ref, halo_rows)] + [(ref, 0) for ref in others[1:]]
    lay_rows(row_ref, pieces, far, far * SUBS,
             lambda ref, base: ref[pl.ds(pl.multiple_of(base + me * SUBS, SUBS), SUBS), :])
    depth = row_ref.shape[0] - 1
    chunk = tiles * SUBS

    def one(chan, carry):
        high_t, low_t = split(toeplitz(row_of(row_ref, chan)))
        moved = {}
        for k in range(tiles):
            value = g_ref[pl.ds(k * SUBS + chan, blocks, stride=chunk), :]
            for steps in range((depth + tiles - 2) // tiles + 1):
                moved[k, steps] = jnp.concatenate(split(shifted(value, steps)), axis=0)
        columns = []
        for d in range(depth):
            parts = []
            for k in range(tiles):
                turns, at = divmod(k + d, tiles)
                parts.append(moved[at, turns])
            columns.append(jnp.concatenate(parts, axis=0))
        left = jnp.concatenate(columns, axis=1)
        right = jnp.concatenate([high_t, low_t], axis=0)
        total = lax.dot_general(left, right, (((1,), (1,)), ((), ())), preferred_element_type=jnp.float32)
        total = total[:, :LANES] + total[:, LANES:]
        for k in range(tiles):
            base = 2 * blocks * k
            value = total[base:base + blocks] + total[base + blocks:base + 2 * blocks]
            held_ref[pl.ds(k * SUBS + chan, blocks, stride=chunk), :] = value
        return carry

    lax.fori_loop(0, SUBS, one, 0, unroll=8)
    for tile in range(blocks * tiles):
        out_ref[:, tile * LANES:(tile + 1) * LANES] = held_ref[tile * SUBS:(tile + 1) * SUBS, :]


def call(body, shapes, scratch=(), flops=0, moved=0, operands=0, after=0, room=40):
    specs = [pl.BlockSpec(memory_space=pltpu.VMEM)] * operands + [pl.BlockSpec(memory_space=pl.ANY)] * after
    shapes = [jax.ShapeDtypeStruct(shape, jnp.float32) for shape in shapes]
    return pl.pallas_call(
        body,
        out_shape=shapes if len(shapes) > 1 else shapes[0],
        **({"in_specs": specs} if specs else {}),
        scratch_shapes=list(scratch),
        compiler_params=pltpu.CompilerParams(vmem_limit_bytes=room * 1024 * 1024),
        cost_estimate=pl.CostEstimate(flops=flops, bytes_accessed=moved, transcendentals=0),
    )


def local(inputs, cotangent, filter_rows, skip_gain, band_blocks):
    far = lax.axis_size("far")
    near = lax.axis_size("near")
    count = far * near
    block_len, chans = inputs.shape
    rows = filter_rows.shape[0]
    tiles = block_len // LANES
    lag_tiles = rows * count // LANES
    halo_blocks = rows * count // block_len
    size = block_len * chans * 4

    def ahead(value, steps):
        return lax.ppermute(value, "far", [(z, (z + steps) % far) for z in range(far)])

    def swapped(parts, order):
        pairs = [[(n, n ^ bits) for n in range(near)] for bits in range(near)]
        return [lax.ppermute(part, "near", pairs[bits]) if bits else part for bits, part in zip(order, parts)]

    share = (far * tiles + far // 2, SUBS, LANES)
    sent_x = call(pack_with_taps, [share] * near, [pltpu.VMEM((near, *share), jnp.float32)], moved=2 * size, room=60)(
        inputs, filter_rows, skip_gain[None, :], band_blocks[None, :])
    got_x = swapped(sent_x, IN_ORDER)
    sent_g, got_x[0] = call(pack_plain, [(count, tiles, SUBS, LANES), share], moved=2 * size)(cotangent, sent_x[0])
    halo_rows = halo_blocks * far * tiles * SUBS
    own_taps = lag_tiles // far * far * SUBS
    halo, taps = call(lambda *refs: collect(rows, halo_blocks, tiles, *refs),
                      [(halo_rows + own_taps, LANES), (own_taps, LANES)],
                      [pltpu.VMEM((near, *share), jnp.float32)], moved=size)(*got_x)
    got_halo = ahead(halo, 1)
    pieces = [taps] + [ahead(taps, steps) for steps in range(2, far)]
    got_g = lax.all_to_all(sent_g, ("far", "near"), split_axis=0, concat_axis=0, tiled=True).reshape(-1, LANES)

    def row(height):
        return pltpu.VMEM((lag_tiles + 2, height, LANES), jnp.float32)

    all_rows = pltpu.VMEM((count * tiles * SUBS, LANES), jnp.float32)
    held_rows = (near + halo_blocks) * share[0] * SUBS
    flops = 2 * far * SUBS * 2 * near * tiles * (lag_tiles + 1) * LANES * 2 * LANES
    share = (far * tiles, SUBS, LANES)
    got_y = swapped(call(lambda *refs: forward(halo_blocks, tiles, near, far, *refs), [share] * near,
                         [all_rows, row(far * SUBS), pltpu.VMEM((held_rows, LANES), jnp.float32)], 40 * flops, 2 * size)(
        *got_x, got_halo, *pieces), OUT_ORDER)
    input_grad, token = call(lambda *refs: gradient(count, tiles, halo_rows, *refs),
                             [(SUBS, count * block_len), (SUBS, LANES)],
                             [row(SUBS), all_rows], flops, 3 * size)(got_g, got_halo, *pieces)
    outputs = call(unpack, [(block_len, chans)], [pltpu.VMEM((near, *share), jnp.float32)], moved=2 * size,
                   operands=near, after=1)(*got_y, token)
    return outputs, input_grad


def solution(mesh):
    count, width = mesh.devices.shape
    fine = Mesh(mesh.devices.reshape(count // NEAR, NEAR, width), ("far", "near", "ch"))
    tokens = ("far", "near")
    return jax.shard_map(
        local,
        mesh=fine,
        in_specs=(P(tokens, "ch"), P(tokens, "ch"), P(tokens, "ch"), P("ch"), P("ch")),
        out_specs=(P(tokens, "ch"), P(("ch", "far", "near"), None)),
        check_vma=False,
    )
```

```python
import jax
import jax.numpy as jnp
from jax import lax
from jax.experimental import pallas as pl
from jax.experimental.pallas import tpu as pltpu
from jax.sharding import Mesh, PartitionSpec as P

LANES = 128
SUBS = 8
NEAR = 8
IN_ORDER = (0, 4, 5, 2, 6, 3, 7, 1)
OUT_ORDER = (0, 1, 2, 4, 6, 5, 3, 7)


def pack_with_taps(x_ref, taps_ref, gain_ref, band_ref, *refs):
    outs, held_ref = refs[:-1], refs[-1]
    block_len, chans = x_ref.shape
    tiles = block_len // LANES
    far = chans // (NEAR * SUBS)
    step = NEAR * SUBS
    for k in range(tiles):
        part = x_ref[k * LANES:(k + 1) * LANES, :].T
        for z in range(far):
            held_ref[:, z * tiles + k, :, :] = part[z * step:(z + 1) * step].reshape(-1, SUBS, LANES)
    rows = taps_ref.shape[0]
    place = lax.axis_index("far") * NEAR + lax.axis_index("near")
    lag = place * rows + lax.broadcasted_iota(jnp.int32, (rows, chans), 0)
    kept = jnp.where(lag < band_ref[...] * block_len, taps_ref[...], 0.0)
    kept = kept + jnp.where(lag == 0, gain_ref[...], 0.0)
    kept = jnp.concatenate([kept, jnp.zeros((LANES - rows, chans), jnp.float32)], axis=0).T
    for pair in range(far // 2):
        low, high = (kept[z * step:(z + 1) * step] for z in (2 * pair, 2 * pair + 1))
        both = low + pltpu.roll(high, LANES // 2, axis=1)
        held_ref[:, far * tiles + pair, :, :] = both.reshape(-1, SUBS, LANES)
    for bits, out_ref in zip(IN_ORDER, outs):
        out_ref[...] = held_ref[other(bits)]


def other(bits):
    return lax.axis_index("near") ^ bits


def merge(order, parts, held_ref):
    for bits, ref in zip(order, parts):
        held_ref[other(bits)] = ref[...]


def pack_plain(g_ref, own_ref, out_ref, same_ref):
    for k in range(g_ref.shape[0] // LANES):
        part = g_ref[k * LANES:(k + 1) * LANES, :].T
        out_ref[:, k, :, :] = part.reshape(-1, SUBS, LANES)
    same_ref[...] = own_ref[...]


def unpack(*refs):
    parts, (out_ref, held_ref) = refs[:NEAR], refs[-2:]
    merge(OUT_ORDER, parts, held_ref)
    tiles = out_ref.shape[0] // LANES
    for k in range(tiles):
        picked = [held_ref[:, at, :, :].reshape(-1, LANES) for at in range(k, held_ref.shape[1], tiles)]
        out_ref[k * LANES:(k + 1) * LANES, :] = jnp.concatenate(picked, axis=0).T


def split(value):
    high = value.astype(jnp.bfloat16)
    return high, (value - high.astype(jnp.float32)).astype(jnp.bfloat16)


def collect(rows, halo_blocks, tiles, *refs):
    parts, (halo_ref, taps_ref, x_ref) = refs[:-3], refs[-3:]
    merge(IN_ORDER, parts, x_ref)
    near = len(parts)
    x_tiles = x_ref.shape[1] * 2 * tiles // (2 * tiles + 1)
    far = x_tiles // tiles
    height = far * SUBS
    lane = lax.broadcasted_iota(jnp.int32, (height, LANES), 1)
    own_tiles = rows * near // LANES
    held = [jnp.zeros((height, LANES), jnp.float32) for _ in range(own_tiles)]
    for piece in range(near):
        tile, offset = divmod(rows * piece, LANES)
        values = []
        for pair in range(far // 2):
            both = x_ref[piece, x_tiles + pair]
            values += [both, pltpu.roll(both, LANES // 2, axis=1)]
        value = jnp.concatenate(values, axis=0)
        turned = pltpu.roll(value, offset, axis=1) if offset else value
        held[tile] = held[tile] + jnp.where((lane >= offset) & (lane < offset + rows), turned, 0.0)
        if offset + rows > LANES:
            held[tile + 1] = held[tile + 1] + jnp.where(lane < offset + rows - LANES, turned, 0.0)
    share = x_tiles * SUBS
    halo_rows = halo_blocks * share
    for tile in range(own_tiles):
        taps_ref[tile * height:(tile + 1) * height, :] = held[tile]
        halo_ref[halo_rows + tile * height:halo_rows + (tile + 1) * height, :] = held[tile]
    for block in range(halo_blocks):
        halo_ref[block * share:(block + 1) * share, :] = x_ref[near - halo_blocks + block, :x_tiles].reshape(share, LANES)


def toeplitz(row):
    wide = jnp.broadcast_to(row, (LANES, row.shape[1]))
    return pltpu.roll(wide, 0, axis=1, stride=1, stride_axis=0)[:, LANES:]


def shifted(value, steps):
    if steps == 0:
        return value
    blank = jnp.zeros((steps, value.shape[1]), value.dtype)
    return jnp.concatenate([value[steps:], blank], axis=0)


def lay_rows(row_ref, pieces, count, height, rows_of):
    per = (row_ref.shape[0] - 2) // count
    row_ref[0] = jnp.zeros(row_ref.shape[1:], jnp.float32)
    row_ref[row_ref.shape[0] - 1] = jnp.zeros(row_ref.shape[1:], jnp.float32)
    me = lax.axis_index("far")
    for back, (ref, base) in enumerate(pieces):
        source = lax.rem(me + count - back, count)
        for tile in range(per):
            row_ref[1 + source * per + tile] = rows_of(ref, base + tile * height)


def row_of(row_ref, chan):
    return jnp.concatenate([row_ref[t, pl.ds(chan, 1), :] for t in range(row_ref.shape[0])], axis=1)


def forward(halo_blocks, tiles, near, far, *refs):
    parts, halo_ref, others, outs = refs[:near], refs[near], refs[near + 1:near + far], refs[near + far:-3]
    y_ref, row_ref, held_ref = refs[-3:]
    chans = far * SUBS
    chunk = parts[0].shape[0] * SUBS
    halo_rows = halo_blocks * far * tiles * SUBS
    pieces = [(others[0], 0), (halo_ref, halo_rows)] + [(ref, 0) for ref in others[1:]]
    lay_rows(row_ref, pieces, far, chans, lambda ref, base: ref[base:base + chans, :])
    first = lax.axis_index("far") == 0
    share = far * tiles * SUBS
    for block in range(halo_blocks):
        value = halo_ref[block * share:(block + 1) * share, :]
        held_ref[block * chunk:block * chunk + share, :] = jnp.where(first, 0.0, value)
    for bits, ref in zip(IN_ORDER, parts):
        at = pl.multiple_of((halo_blocks + other(bits)) * chunk, SUBS)
        held_ref[pl.ds(at, chunk), :] = ref[...].reshape(chunk, LANES)
    depth = row_ref.shape[0] - 1

    def one(chan, carry):
        z, i = lax.div(chan, SUBS), lax.rem(chan, SUBS)
        high_t, low_t = split(toeplitz(row_of(row_ref, chan)))
        moved = {}
        for k in range(tiles):
            for steps in range(halo_blocks + 1):
                start = (halo_blocks - steps) * chunk + (z * tiles + k) * SUBS + i
                moved[k, steps] = jnp.concatenate(split(held_ref[pl.ds(start, near, stride=chunk), :]), axis=0)
        columns = []
        for d in range(depth):
            parts = []
            for k in range(tiles):
                turns, at = divmod(k - d, tiles)
                parts.append(moved[at, -turns])
            columns.append(jnp.concatenate(parts, axis=0))
        left = jnp.concatenate(columns, axis=1)
        right = jnp.concatenate(
            [jnp.concatenate([t[:, d * LANES:(d + 1) * LANES] for t in (high_t, low_t)], axis=1) for d in range(depth)],
            axis=0,
        )
        total = jnp.dot(left, right, preferred_element_type=jnp.float32)
        total = total[:, :LANES] + total[:, LANES:]
        for k in range(tiles):
            base = 2 * near * k
            value = total[base:base + near] + total[base + near:base + 2 * near]
            y_ref[pl.ds((z * tiles + k) * SUBS + i, near, stride=far * tiles * SUBS), :] = value
        return carry

    lax.fori_loop(0, chans, one, 0, unroll=32)
    for bits, ref in zip(OUT_ORDER, outs):
        at = pl.multiple_of(other(bits) * share, SUBS)
        ref[...] = y_ref[pl.ds(at, share), :].reshape(ref.shape)


def gradient(blocks, tiles, halo_rows, g_ref, halo_ref, *refs):
    others, (out_ref, token_ref, row_ref, held_ref) = refs[:-4], refs[-4:]
    token_ref[...] = jnp.zeros(token_ref.shape, jnp.float32)
    far = len(others) + 1
    me = lax.axis_index("far")
    pieces = [(others[0], 0), (halo_ref, halo_rows)] + [(ref, 0) for ref in others[1:]]
    lay_rows(row_ref, pieces, far, far * SUBS,
             lambda ref, base: ref[pl.ds(pl.multiple_of(base + me * SUBS, SUBS), SUBS), :])
    depth = row_ref.shape[0] - 1
    chunk = tiles * SUBS

    def one(chan, carry):
        high_t, low_t = split(toeplitz(row_of(row_ref, chan)))
        moved = {}
        for k in range(tiles):
            value = g_ref[pl.ds(k * SUBS + chan, blocks, stride=chunk), :]
            for steps in range((depth + tiles - 2) // tiles + 1):
                moved[k, steps] = jnp.concatenate(split(shifted(value, steps)), axis=0)
        columns = []
        for d in range(depth):
            parts = []
            for k in range(tiles):
                turns, at = divmod(k + d, tiles)
                parts.append(moved[at, turns])
            columns.append(jnp.concatenate(parts, axis=0))
        left = jnp.concatenate(columns, axis=1)
        right = jnp.concatenate([high_t, low_t], axis=0)
        total = lax.dot_general(left, right, (((1,), (1,)), ((), ())), preferred_element_type=jnp.float32)
        total = total[:, :LANES] + total[:, LANES:]
        for k in range(tiles):
            base = 2 * blocks * k
            value = total[base:base + blocks] + total[base + blocks:base + 2 * blocks]
            held_ref[pl.ds(k * SUBS + chan, blocks, stride=chunk), :] = value
        return carry

    lax.fori_loop(0, SUBS, one, 0, unroll=8)
    for tile in range(blocks * tiles):
        out_ref[:, tile * LANES:(tile + 1) * LANES] = held_ref[tile * SUBS:(tile + 1) * SUBS, :]


def call(body, shapes, scratch=(), flops=0, moved=0, operands=0, after=0, room=40):
    specs = [pl.BlockSpec(memory_space=pltpu.VMEM)] * operands + [pl.BlockSpec(memory_space=pl.ANY)] * after
    shapes = [jax.ShapeDtypeStruct(shape, jnp.float32) for shape in shapes]
    return pl.pallas_call(
        body,
        out_shape=shapes if len(shapes) > 1 else shapes[0],
        **({"in_specs": specs} if specs else {}),
        scratch_shapes=list(scratch),
        compiler_params=pltpu.CompilerParams(vmem_limit_bytes=room * 1024 * 1024),
        cost_estimate=pl.CostEstimate(flops=flops, bytes_accessed=moved, transcendentals=0),
    )


def local(inputs, cotangent, filter_rows, skip_gain, band_blocks):
    far = lax.axis_size("far")
    near = lax.axis_size("near")
    count = far * near
    block_len, chans = inputs.shape
    rows = filter_rows.shape[0]
    tiles = block_len // LANES
    lag_tiles = rows * count // LANES
    halo_blocks = rows * count // block_len
    size = block_len * chans * 4

    def ahead(value, steps):
        return lax.ppermute(value, "far", [(z, (z + steps) % far) for z in range(far)])

    def swapped(parts, order):
        pairs = [[(n, n ^ bits) for n in range(near)] for bits in range(near)]
        return [lax.ppermute(part, "near", pairs[bits]) if bits else part for bits, part in zip(order, parts)]

    share = (far * tiles + far // 2, SUBS, LANES)
    sent_x = call(pack_with_taps, [share] * near, [pltpu.VMEM((near, *share), jnp.float32)], moved=2 * size, room=60)(
        inputs, filter_rows, skip_gain[None, :], band_blocks[None, :])
    got_x = swapped(sent_x, IN_ORDER)
    sent_g, got_x[0] = call(pack_plain, [(count, tiles, SUBS, LANES), share], moved=2 * size)(cotangent, sent_x[0])
    halo_rows = halo_blocks * far * tiles * SUBS
    own_taps = lag_tiles // far * far * SUBS
    halo, taps = call(lambda *refs: collect(rows, halo_blocks, tiles, *refs),
                      [(halo_rows + own_taps, LANES), (own_taps, LANES)],
                      [pltpu.VMEM((near, *share), jnp.float32)], moved=size)(*got_x)
    got_halo = ahead(halo, 1)
    pieces = [taps] + [ahead(taps, steps) for steps in range(2, far)]
    got_g = lax.all_to_all(sent_g, ("far", "near"), split_axis=0, concat_axis=0, tiled=True).reshape(-1, LANES)

    def row(height):
        return pltpu.VMEM((lag_tiles + 2, height, LANES), jnp.float32)

    all_rows = pltpu.VMEM((count * tiles * SUBS, LANES), jnp.float32)
    held_rows = (near + halo_blocks) * share[0] * SUBS
    flops = 2 * far * SUBS * 2 * near * tiles * (lag_tiles + 1) * LANES * 2 * LANES
    share = (far * tiles, SUBS, LANES)
    got_y = swapped(call(lambda *refs: forward(halo_blocks, tiles, near, far, *refs), [share] * near,
                         [all_rows, row(far * SUBS), pltpu.VMEM((held_rows, LANES), jnp.float32)], 40 * flops, 2 * size)(
        *got_x, got_halo, *pieces), OUT_ORDER)
    input_grad, token = call(lambda *refs: gradient(count, tiles, halo_rows, *refs),
                             [(SUBS, count * block_len), (SUBS, LANES)],
                             [row(SUBS), all_rows], flops, 3 * size)(got_g, got_halo, *pieces)
    outputs = call(unpack, [(block_len, chans)], [pltpu.VMEM((near, *share), jnp.float32)], moved=2 * size,
                   operands=near, after=1)(*got_y, token)
    return outputs, input_grad


def solution(mesh):
    count, width = mesh.devices.shape
    fine = Mesh(mesh.devices.reshape(count // NEAR, NEAR, width), ("far", "near", "ch"))
    tokens = ("far", "near")
    return jax.shard_map(
        local,
        mesh=fine,
        in_specs=(P(tokens, "ch"), P(tokens, "ch"), P(tokens, "ch"), P("ch"), P("ch")),
        out_specs=(P(tokens, "ch"), P(("ch", "far", "near"), None)),
        check_vma=False,
    )
```
